128 devices in a mesh: seq: 16 (over z, y), head: 8 (over x, core).
Axes of the slice: x: 4, y: 4, z: 4, core: 2. Of those that a mesh axis runs over, the one named last changes fastest.
Arguments:
- prompt_hidden: bfloat16 [16384, 7168], P('seq', 'head'), may hold values from -6 to 6
- owner: int32 [16384, 1], P('seq'), may hold values from 0 to 15; in each aligned block of 1024 rows (0 to 1023, 1024 to 2047, ...) at most 128 rows name the same one
- offsets: int32 [16384], P('seq'), may hold values from 0 to 16383, as said below
- cache: bfloat16 [256, 1024, 576], P('seq')
- lengths: int32 [256], P('seq'), may hold values from 1 to 1022, 131072 in all
- new_hidden: bfloat16 [2, 256, 7168], P(None, 'seq', 'head'), may hold values from -6 to 6
- w_down: bfloat16 [7168, 2112], P('head'), may hold values from -0.0625 to 0.0625
- gain_q: bfloat16 [1536], replicated, may hold values from 0.099609375 to 1.8984375
- gain_kv: bfloat16 [512], replicated, may hold values from 0.099609375 to 1.8984375
- w_uq: bfloat16 [1536, 24576], P(None, 'head'), may hold values from -0.15625 to 0.15625
- w_uk: bfloat16 [128, 128, 512], P('head'), may hold values from -0.5 to 0.5
- w_uv: bfloat16 [128, 512, 128], P('head'), may hold values from -0.25 to 0.25
- w_out: bfloat16 [16384, 7168], P('head', 'seq'), may hold values from -0.046875 to 0.046875
Outputs:
- attended: bfloat16 [2, 256, 7168], P(None, 'head', 'seq')
The draws below stay inside these ranges and needn't reach their ends.
Inputs may be any that keep to these rules, and one draw needn't show every extreme that they name: offsets are distinct over all prompt tokens. Among the rows of one index of seq at most 128 name one owner.
All inputs are finite; a program needn't handle non-finite values. No bound on the sum of `lengths` on one device may be relied on, other than what follows from the above.
Results may differ from the reference program's by a relative error of at most 0.03.
Values may be sent and summed in bfloat16 or wider, within the bound.
A program may use at most 256 MiB of HBM per device.

```python
import math
import jax
import jax.numpy as jnp
import numpy as np
from jax import lax

D = 7168
H = 128
QRANK = 1536
LATENT = 512
ROPE = 64
NOPE = 128
VDIM = 128
STEPS = 2
TOK_DEV = 1024
REQ_DEV = 16
CACHE = 1024
TOKENS = 16384
REQUESTS = 256
CAP = 128
N_SEQ = 16


def draw_offsets(key, part):
    key = jax.random.fold_in(key, 11)
    order = jax.random.permutation(key, REQ_DEV * CACHE)
    return order[:TOKENS].astype(jnp.int32)


def draw_cache(key, part):
    key = jax.random.fold_in(key, 23)
    first = jax.random.fold_in(key, 0)
    shape = (REQUESTS, CACHE, LATENT + ROPE)
    values = jax.random.normal(first, shape, jnp.float32)
    return values.astype(jnp.bfloat16)


def block_levels(rng, extent, cuts, smallest, largest):
    factor_of = 1.0
    for axis_at, parts in cuts:
        draws = jax.random.uniform(jax.random.fold_in(jax.random.fold_in(rng, 6), axis_at), (parts,), jnp.float32, smallest / len(cuts), largest / len(cuts))
        factor_of = factor_of * jnp.repeat(jnp.exp(draws), extent[axis_at] // parts).reshape((-1,) + (1,) * (len(extent) - 1 - axis_at))
    return factor_of


def split_up(count, total, most, slope):
    loads = [(1 << 20) // math.isqrt(rank ** slope) + 1 for rank in range(2, count + 1)]
    spare, counts = total - most - (count - 1), [1] * (count - 1)
    while spare > 0:
        movable = [i for i in range(count - 1) if counts[i] < most]
        pool, remaining = sum([loads[i] for i in movable]), spare
        for i in movable:
            extra = min(most - counts[i], max(1, remaining * loads[i] // pool), spare)
            counts[i] = counts[i] + extra
            spare = spare - extra
    return np.array([most] + counts)


def ragged_sizes(rng, number_of, total, most, skew):
    if number_of == 2:
        one = jax.random.randint(rng, (), max(1, total - most), min(most, total - 1) + 1)
        return jnp.stack([one, total - one])
    sizes = jnp.asarray(split_up(number_of, total, most, skew), jnp.int32)
    couples = (number_of - 1) // 2
    donor, receiver = sizes[1:1 + 2 * couples:2], sizes[2:2 + 2 * couples:2]
    room = jnp.minimum(donor - 1, most - receiver)
    moved = jax.random.randint(jax.random.fold_in(rng, 1), (couples,), 0, 1 << 20) % (room + 1)
    sizes = sizes.at[1:1 + 2 * couples:2].set(donor - moved).at[2:2 + 2 * couples:2].set(receiver + moved)
    return sizes[jax.random.permutation(jax.random.fold_in(rng, 2), number_of)]


def deal_out(key, own, number, rows, amount, top, limit, slope):
    order = jax.random.permutation(key, amount)
    crowded, common = load_shares(amount, rows * top, limit, slope, True), load_shares(amount, rows * top, limit, slope, False)
    places = jnp.arange(amount)

    def named(tallies, turn):
        used = int((tallies > 0).sum())
        fixed = max(1, used // 4)
        passed = fixed + (places - fixed + turn * (used - fixed)) % max(1, amount - fixed)
        return jnp.zeros((amount,), jnp.int32).at[order[jnp.where(places < fixed, places, passed)]].set(jnp.asarray(tallies, jnp.int32))

    tallies = jnp.where(number % 4 == 0, named(crowded, number // 4), named(common, number - number // 4 - 1))
    mixed = jax.random.permutation(jax.random.fold_in(own, 3), amount)
    source_of, receiver = mixed[0:amount // 2 * 2:2], mixed[1:amount // 2 * 2:2]
    slack = jnp.minimum(tallies[source_of] - 1, limit - tallies[receiver]) // 2
    slack = jnp.where((source_of == order[0]) | (receiver == order[0]) | (tallies[receiver] == 0), 0, jnp.maximum(slack, 0))
    passed = jax.random.randint(jax.random.fold_in(own, 4), (amount // 2,), 0, 1 << 20) % (slack + 1)
    tallies = tallies.at[source_of].add(-passed).at[receiver].add(passed)
    members = jnp.searchsorted(jnp.cumsum(tallies), jnp.arange(rows * top), side="right").astype(jnp.int32)
    table = members.reshape(top, rows).T
    table = table[jax.random.permutation(jax.random.fold_in(own, 1), rows)]
    turn = jax.random.randint(jax.random.fold_in(own, 2), (rows, 1), 0, top)
    return jnp.take_along_axis(table, (jnp.arange(top)[None, :] + turn) % top, axis=1)


def load_shares(number_of, total, most, skew, full):
    loads = [(1 << 20) // math.isqrt(grade ** skew) + 1 for grade in range(1, number_of + 1)]
    largest = most if full else min(most, max(-(-total // number_of), total * loads[0] // sum(loads)))
    least = 1 if total - largest >= number_of - 1 else 0
    counts, spare = [largest] + [least] * (number_of - 1), total - largest - least * (number_of - 1)
    while spare > 0:
        candidates = [i for i in range(1, number_of) if counts[i] < largest] or [i for i in range(1, number_of) if counts[i] < most]
        mass, budget = sum([loads[i] for i in candidates]), spare
        for i in candidates:
            more = min(most - counts[i], max(1, budget * loads[i] // mass), spare)
            counts[i] = counts[i] + more
            spare = spare - more
    return np.array(counts)


def scatter_about(stream_key, dims, spread, most, shards=(), kind=jnp.bfloat16):
    values = jax.random.normal(stream_key, dims, jnp.float32) * spread
    if len(shards) > 0:
        values = block_levels(stream_key, dims, shards, -0.22, 0.18) * values
    return jnp.clip(values, min=-most, max=most).astype(kind)


def setup_inputs(seed: int = 0) -> dict:
    key_list = jax.random.split(jax.random.key(seed), 14)
    prompt_hidden = scatter_about(key_list[0], (TOKENS, D), 1.0, 6.0, ((0, 16), (1, 8)))
    owner_keys = jax.random.split(jax.random.fold_in(key_list[1], 1), TOKENS // TOK_DEV)
    owner_turns = jax.random.permutation(jax.random.fold_in(key_list[1], 3), TOKENS // TOK_DEV)
    owner = jax.vmap(lambda own, number: deal_out(jax.random.fold_in(key_list[1], 2), own, number, TOK_DEV, N_SEQ, 1, CAP, 2))(owner_keys, owner_turns).reshape((TOKENS, 1))
    offsets = draw_offsets(jax.random.fold_in(key_list[13], 71), 0)
    cache = draw_cache(jax.random.fold_in(key_list[13], 71), 0)
    lengths = ragged_sizes(key_list[4], REQUESTS, REQUESTS * CACHE // 2, CACHE - 2, 2).astype(jnp.int32)
    new_hidden = scatter_about(key_list[5], (STEPS, REQUESTS, D), 1.0, 6.0, ((1, 16), (2, 8)))
    w_down = scatter_about(key_list[6], (D, QRANK + LATENT + ROPE), D ** -0.5, 0.0625, ((0, 8),))
    gain_q = jnp.clip(1.0 + 0.18 * jax.random.normal(key_list[7], (QRANK,), jnp.float32), 0.099609375, 1.8984375).astype(jnp.bfloat16)
    gain_kv = jnp.clip(1.0 + 0.18 * jax.random.normal(key_list[8], (LATENT,), jnp.float32), 0.099609375, 1.8984375).astype(jnp.bfloat16)
    w_uq = scatter_about(key_list[9], (QRANK, H * (NOPE + ROPE)), QRANK ** -0.5, 0.15625, ((1, 8),))
    w_uk = scatter_about(key_list[10], (H, NOPE, LATENT), NOPE ** -0.5, 0.5, ((0, 8),))
    w_uv = scatter_about(key_list[11], (H, LATENT, VDIM), LATENT ** -0.5, 0.25, ((0, 8),))
    w_out = scatter_about(key_list[12], (H * VDIM, D), (H * VDIM) ** -0.5, 0.046875, ((0, 8), (1, 16)))
    return {"prompt_hidden": prompt_hidden, "owner": owner, "offsets": offsets, "cache": cache, "lengths": lengths, "new_hidden": new_hidden, "w_down": w_down, "gain_q": gain_q, "gain_kv": gain_kv, "w_uq": w_uq, "w_uk": w_uk, "w_uv": w_uv, "w_out": w_out}


def rms_norm(values, gain):
    return values * lax.rsqrt(lax.optimization_barrier(jnp.mean(values * values, -1, keepdims=True)) + 1e-06) * gain.astype(jnp.float32)

def rotate(values, places):
    half = values.shape[-1] // 2
    inverse = 10000.0 ** (-jnp.arange(half, dtype=jnp.float32) / half)
    angles = places.astype(jnp.float32)[..., None] * inverse
    first = values[..., :half]
    second = values[..., half:]
    return jnp.concatenate([first * jnp.cos(angles) - second * jnp.sin(angles), second * jnp.cos(angles) + first * jnp.sin(angles)], -1)

def latent_rows(part, gain_kv, places):
    latent = rms_norm(part[..., :LATENT], gain_kv)
    shared = rotate(part[..., LATENT:], places)
    return jnp.concatenate([latent, shared], -1).astype(jnp.bfloat16)

def reference(prompt_hidden, owner, offsets, cache, lengths, new_hidden, w_down, gain_q, gain_kv, w_uq, w_uk, w_uv, w_out):
    prompt_part = jnp.dot(prompt_hidden, w_down[:, QRANK:], preferred_element_type=jnp.float32)
    prompt_rows = latent_rows(prompt_part, gain_kv, offsets % CACHE)
    width = LATENT + ROPE
    flat = cache.reshape(REQUESTS * CACHE, width)
    target = (owner[:, 0] * (REQ_DEV * CACHE) + offsets).astype(jnp.int32)
    flat = flat.at[target].set(prompt_rows)
    new_part = jnp.dot(new_hidden.reshape(STEPS * REQUESTS, D), w_down, preferred_element_type=jnp.float32)
    new_part = new_part.reshape(STEPS, REQUESTS, -1)
    positions = (lengths[None, :] + jnp.arange(STEPS, dtype=jnp.int32)[:, None]).astype(jnp.int32)
    new_rows = latent_rows(new_part[..., QRANK:], gain_kv, positions)
    request_ids = jnp.broadcast_to(jnp.arange(REQUESTS, dtype=jnp.int32)[None, :], (STEPS, REQUESTS))
    keys = flat.reshape(REQUESTS, CACHE, width).at[request_ids, positions].set(new_rows)
    query_latent = rms_norm(new_part[..., :QRANK], gain_q).astype(jnp.bfloat16)
    query = jnp.dot(query_latent.reshape(STEPS * REQUESTS, QRANK), w_uq, preferred_element_type=jnp.float32)
    query = query.reshape(STEPS, REQUESTS, H, NOPE + ROPE)
    q_nope = query[..., :NOPE].astype(jnp.bfloat16)
    q_rope = rotate(query[..., NOPE:], positions[:, :, None]).astype(jnp.bfloat16)
    q_lat = jnp.einsum('srhn,hnc->srhc', q_nope.astype(jnp.float32), w_uk.astype(jnp.float32)).astype(jnp.bfloat16)
    joined = jnp.concatenate([q_lat, q_rope], -1)
    scores = jnp.einsum('srhc,rlc->srhl', joined.astype(jnp.float32), keys.astype(jnp.float32)) / jnp.sqrt(jnp.float32(NOPE + ROPE))
    visible = jnp.arange(CACHE, dtype=jnp.int32)[None, None, None, :] <= positions[:, :, None, None]
    scores = jnp.where(visible, scores, -jnp.inf)
    top = lax.optimization_barrier(jnp.max(scores, -1, keepdims=True))
    expo = jnp.exp(scores - top)
    weights = (expo / lax.optimization_barrier(jnp.sum(expo, -1, keepdims=True))).astype(jnp.bfloat16)
    o_lat = jnp.einsum('srhl,rlc->srhc', weights.astype(jnp.float32), keys[..., :LATENT].astype(jnp.float32)).astype(jnp.bfloat16)
    heads_out = jnp.einsum('srhc,hcv->srhv', o_lat.astype(jnp.float32), w_uv.astype(jnp.float32)).astype(jnp.bfloat16)
    heads_out = heads_out.reshape(STEPS * REQUESTS, H * VDIM)
    attended = jnp.dot(heads_out, w_out, preferred_element_type=jnp.float32)
    return attended.reshape(STEPS, REQUESTS, D).astype(jnp.bfloat16)
```

```python
import functools

import jax
import jax.numpy as jnp
from jax import lax
from jax.experimental import pallas as pl
from jax.experimental.pallas import tpu as pltpu
from jax.sharding import PartitionSpec as P

F32 = jnp.float32
BF16 = jnp.bfloat16
I32 = jnp.int32
MESH = pl.DeviceIdType.MESH
QRANK = 1536
LATENT = 512
ROPE = 64
NOPE = 128
VDIM = 128
HIDE = -1e30
LOG2E = 1.4426950408889634


def nt(a, b):
    return lax.dot_general(a, b, (((1,), (1,)), ((), ())), preferred_element_type=F32)


def nn(a, b):
    return jnp.dot(a, b, preferred_element_type=F32)


def iota(shape, dim):
    return lax.broadcasted_iota(I32, shape, dim)


def one_hot(cond):
    return jnp.where(cond, 1.0, 0.0).astype(BF16)


def kernel(
    own_r, off_r, ctab, ex, ntab, nex, qex, vis, wrow, gq, gkv, newh,
    hid_h, wd_h, uq_h, uk_h, cache_h, uv_h, wo_h,
    out,
    hid, wd, uq, uk, kc, uv, wo, lsem, ksem,
    rs, tsend, trecv, ts_sem, tr_sem,
    npp, npair, npx, npxr, npfin, np_ss, np_rs,
    wr, part, ps, pr, xs, xr, mine, p_ss, p_rs, x_ss, x_rs,
    disp, slots, d_ss, d_rs, g_ss, g_rs,
    qls, ql, qs, newk, biasm, acc, m_s, l_s, ob, op,
    hog, h_ss, h_rs, osend, orecv, o_ss, o_rs,
):
    i = lax.axis_index("seq")
    j = lax.axis_index("head")
    x = j // 2
    c = j % 2
    z = i // 4
    y = i % 4
    sib = 2 * x + (1 - c)

    def load(src, dst, sem):
        cp = pltpu.make_async_copy(src, dst, sem)
        cp.start()
        return cp

    def remote(src, dst, ss, rr, dev):
        return pltpu.make_async_remote_copy(
            src_ref=src, dst_ref=dst, send_sem=ss, recv_sem=rr,
            device_id=dev, device_id_type=MESH,
        )

    c_wd = load(wd_h, wd, lsem.at[0])
    c_hid = load(hid_h, hid, lsem.at[1])

    barrier = pltpu.get_barrier_semaphore()
    for dj in range(1, 8):
        pl.semaphore_signal(barrier, inc=1, device_id=(i, (j + dj) % 8), device_id_type=MESH)
    for di in range(1, 16):
        pl.semaphore_signal(barrier, inc=1, device_id=((i + di) % 16, j), device_id_type=MESH)

    sub128 = iota((128, 128), 0)
    lane128 = iota((128, 128), 1)
    upper = one_hot(sub128 < lane128)
    sub16 = iota((16, 128), 0)
    hots, pres = [], []
    count = jnp.zeros((16, 1), F32)
    for b in range(8):
        hot = jnp.where(sub16 == own_r[b : b + 1, :], 1.0, 0.0)
        pres.append(nn(hot.astype(BF16), upper) + count)
        hots.append(hot)
        count = count + jnp.sum(hot, axis=1, keepdims=True)
    count = jnp.broadcast_to(count, (16, 128))
    start = jnp.zeros((16, 128), F32)
    for o in range(15):
        start = start + jnp.where(sub16 > o, count[o : o + 1, :], 0.0)
    table = jnp.zeros((48, 128), F32)
    for b in range(8):
        place = jnp.sum(hots[b] * (pres[b] + start), axis=0, keepdims=True).astype(I32)
        dev = place & 7
        at = place >> 3
        rs[b : b + 1, :] = dev * 128 + at
        key = dev * 16 + (at & 15)
        off = off_r[b : b + 1, :]
        high = (off >> 7).astype(F32)
        low = (off & 127).astype(F32)
        digits = jnp.concatenate([hots[b] * high, hots[b] * low, hots[b]], axis=0).astype(BF16)
        table = table + nt(digits, one_hot(sub128 == key))
    cells = jnp.where(table[32:48] > 0.5, table[0:16] * 128.0 + table[16:32], -1.0)
    for o in range(16):
        tsend[o] = jnp.broadcast_to(cells[o : o + 1, :], (8, 128))
    row_place = (iota((16, 128), 1) * 8 + j).astype(F32)
    owner_at = jnp.sum(
        jnp.where(row_place >= start + count, 1.0, 0.0), axis=0, keepdims=True
    ).astype(I32)
    slot_at = owner_at * 16 + (iota((1, 128), 1) & 15)
    rs[8:9, :] = slot_at

    pl.semaphore_wait(barrier, 22)

    def t_copy(di):
        to = (i + di) % 16
        return remote(tsend.at[to], trecv.at[i], ts_sem.at[di], tr_sem.at[di], (to, j))

    for di in range(1, 16):
        t_copy(di).start()

    c_wd.wait()
    c_uq = load(uq_h, uq, lsem.at[2])
    c_uk = load(uk_h, uk, lsem.at[3])
    wr[0:64, :] = wd[2048:2112, :]
    wr[64:96, :] = wd[2080:2112, :]
    wr[96:128, :] = wd[2048:2080, :]
    npp[0] = nt(newh[...], wd[0:1152, :]).astype(BF16)
    npp[1, :, 0:896] = nt(newh[...], wd[1152:2048, :]).astype(BF16)
    npp[1, :, 896:1024] = nt(newh[...], wr[...]).astype(BF16)
    npp[1, :, 1024:1152] = jnp.zeros((32, 128), BF16)
    np_pair = remote(npp.at[1 - c], npair, np_ss.at[0], np_rs.at[0], (i, sib))
    np_pair.start()

    c_hid.wait()

    def k_copy(r):
        return pltpu.make_async_copy(cache_h.at[r], kc.at[r], ksem.at[r])

    @pl.loop(0, 16)
    def _(r):
        k_copy(r).start()

    c_uv = load(uv_h, uv, lsem.at[4])
    c_wo = load(wo_h, wo, lsem.at[5])
    low_lane = iota((256, 128), 1) < 64

    @pl.loop(0, 4)
    def _(t):
        rows = pl.ds(pl.multiple_of(t * 256, 256), 256)
        h = hid[rows, :]
        part[rows, 0:512] = nt(h, wd[1536:2048, :]).astype(BF16)
        u = nt(h, wr[...]) * ctab[rows, :]
        u = u + pltpu.roll(u, 64, 1)
        part[rows, 512:640] = jnp.where(low_lane, u, ex[rows, :].astype(F32)).astype(BF16)

    def permuted(first, second):
        ids = rs[0:8, :]
        top = [one_hot(sub128 == ids[b : b + 1, :] - first * 128) for b in range(8)]
        low = [one_hot(sub128 == ids[b : b + 1, :] - second * 128) for b in range(8)]
        pick = jnp.concatenate(
            [jnp.concatenate(top, axis=1), jnp.concatenate(low, axis=1)], axis=0
        )
        return nn(pick, part[...])

    def p_copy(dx):
        return remote(ps.at[dx], pr.at[dx], p_ss.at[dx], p_rs.at[dx], (i, sib))

    for first, second in ((2, 1), (3, 0)):
        both = permuted(2 * ((x + first) % 4) + 1 - c, 2 * ((x + second) % 4) + 1 - c)
        ps[first] = both[0:128].astype(BF16)
        ps[second] = both[128:256].astype(BF16)
        p_copy(first).start()
        p_copy(second).start()

    np_pair.wait_recv()
    npx[...] = (npp[c].astype(F32) + npair[...].astype(F32)).astype(BF16)

    def npx_copy(dx):
        return remote(
            npx, npxr.at[dx], np_ss.at[dx], np_rs.at[dx], (i, 2 * ((x + dx) % 4) + c)
        )

    for dx in (2, 1, 3):
        npx_copy(dx).start()

    def x_copy(dx):
        return remote(
            xs.at[dx], xr.at[dx], x_ss.at[dx], x_rs.at[dx], (i, 2 * ((x + dx) % 4) + c)
        )

    for first, second in ((2, 1), (3, 0)):
        both = permuted(2 * ((x + first) % 4) + c, 2 * ((x + second) % 4) + c)
        p_copy(first).wait_recv()
        xs[first] = (both[0:128] + pr[first].astype(F32)).astype(BF16)
        x_copy(first).start()
        p_copy(second).wait_recv()
        if second == 0:
            mine[...] = both[128:256] + pr[0].astype(F32)
        else:
            xs[second] = (both[128:256] + pr[second].astype(F32)).astype(BF16)
            x_copy(second).start()

    total = npx[...].astype(F32)
    for dx in (1, 3, 2):
        npx_copy(dx).wait_recv()
        total = total + npxr[dx].astype(F32)
    npfin[c] = total.astype(BF16)
    np_swap = remote(npfin.at[c], npfin.at[c], np_ss.at[4], np_rs.at[4], (i, sib))
    np_swap.start()
    np_swap_in = remote(npfin.at[1 - c], npfin.at[1 - c], np_ss.at[4], np_rs.at[4], (i, sib))
    np_swap_in.wait_recv()

    low32 = iota((32, 128), 1) < 64
    q_in = jnp.concatenate([npfin[0], npfin[1, :, 0:384]], axis=1).astype(F32)
    q_in = q_in * lax.rsqrt(jnp.mean(q_in * q_in, axis=1, keepdims=True) + 1e-6) * gq[...]
    qls[...] = q_in.astype(BF16)
    k_in = npfin[1, :, 384:896].astype(F32)
    k_in = k_in * lax.rsqrt(jnp.mean(k_in * k_in, axis=1, keepdims=True) + 1e-6) * gkv[...]
    newk[0:32, 0:512] = k_in.astype(BF16)
    newk[32:128, 0:512] = jnp.zeros((96, 512), BF16)
    u = npfin[1, :, 896:1024].astype(F32) * ntab[0]
    u = u + pltpu.roll(u, 64, 1)
    newk[0:32, 512:640] = jnp.where(low32, u, nex[0:32, :]).astype(BF16)
    newk[32:128, 512:640] = nex[32:128, :].astype(BF16)

    c_uq.wait()
    c_uk.wait()
    inner = (iota((32, 128), 1) & 63) < 32

    @pl.loop(0, 8)
    def _(p):
        q = nn(qls[...], uq[:, pl.ds(pl.multiple_of(p * 384, 384), 384)])
        t0, t1, t2 = q[:, 0:128], q[:, 128:256], q[:, 256:384]
        odd = jnp.where(low32, pltpu.roll(t1, 64, 1), pltpu.roll(t2, 64, 1))
        rope = jnp.where(low32, t1, t2)
        turned = jnp.where(inner, pltpu.roll(rope, 96, 1), pltpu.roll(rope, 32, 1))
        rope = rope * ntab[1] + turned * ntab[2]
        for s, (nope, rot) in enumerate(((t0, rope), (odd, pltpu.roll(rope, 64, 1)))):
            rows = pl.ds(pl.multiple_of(p * 64 + s * 32, 32), 32)
            ql[rows, 0:512] = nn(nope.astype(BF16), uk[2 * p + s]).astype(BF16)
            ql[rows, 512:640] = jnp.where(low32, rot, qex[...]).astype(BF16)

    @pl.loop(0, 2)
    def _(t):
        n = iota((256, 512), 0) + t * 256
        want = ((n & 31) >> 1) * 32 + (n & 1) * 16 + (n >> 5)
        rows = pl.ds(pl.multiple_of(t * 256, 256), 256)
        qs[rows, :] = nn(one_hot(iota((256, 512), 1) == want), ql[...]).astype(BF16)

    total = mine[...]
    for dx in (1, 3, 2):
        x_copy(dx).wait_recv()
        total = total + xr[dx].astype(F32)
    lat = total[:, 0:512]
    lat = lat * lax.rsqrt(jnp.mean(lat * lat, axis=1, keepdims=True) + 1e-6) * gkv[...]
    tail = total[:, 512:640]
    tail = jnp.where(iota((128, 128), 1) < 64, tail, tail * 0.125)
    rows_b = jnp.concatenate([lat, tail], axis=1).astype(BF16)
    spread = one_hot(iota((256, 128), 0) == rs[8:9, :])
    disp[...] = nn(spread, rows_b).astype(BF16)

    def d_copy(di):
        to = (i + di) % 16
        return remote(
            disp.at[pl.ds(pl.multiple_of(to * 16, 16), 16), :],
            slots.at[j, pl.ds(pl.multiple_of(i * 16, 16), 16), :],
            d_ss.at[di], d_rs.at[di], (to, j),
        )

    for di in range(1, 16):
        d_copy(di).start()
    at_me = pl.ds(pl.multiple_of(i * 16, 16), 16)
    slots[j, at_me, :] = disp[at_me, :]

    at_src = tsend[i]
    trecv[i] = at_src
    for di in range(1, 16):
        src = (i + 16 - di) % 16
        remote(tsend.at[src], trecv.at[src], ts_sem.at[di], tr_sem.at[di], (src, j)).wait_recv()

    def add_cells(s, total):
        cell = trecv[s, 0:1, :].astype(I32)
        return total + nt(one_hot(sub128 == (cell >> 7)), one_hot(sub128 == (cell & 127)))

    taken = lax.fori_loop(0, 16, add_cells, jnp.zeros((128, 128), F32))
    biasm[...] = jnp.where((taken < 0.5) & (vis[...] > 0.5), 0.0, HIDE)

    unit = LOG2E / (NOPE + ROPE) ** 0.5

    def cache_part(r):
        k_copy(r).wait()
        rows = pl.ds(pl.multiple_of(r * 32, 32), 32)
        s = nn(qs[rows, 0:576], kc[r])
        b8 = biasm[pl.ds(pl.multiple_of(r * 8, 8), 8), :]
        s = s + jnp.concatenate([b8[g : g + 1, :] for g in range(8)], axis=1)
        sn = nt(qs[rows, :], newk[...])
        m = jnp.maximum(jnp.max(s, axis=1, keepdims=True), jnp.max(sn, axis=1, keepdims=True))
        e = jnp.exp2((s - m) * unit)
        en = jnp.exp2((sn - m) * unit)
        l = jnp.sum(e, axis=1, keepdims=True) + jnp.sum(en, axis=1, keepdims=True)
        acc[rows, :] = nt(e.astype(BF16), kc[r, 0:512, :]) + nn(en.astype(BF16), newk[:, 0:512])
        m_s[rows, :] = jnp.broadcast_to(m, (32, 128))
        l_s[rows, :] = jnp.broadcast_to(l, (32, 128))

    @pl.loop(0, 6)
    def _(r):
        cache_part(r)

    for di in range(1, 16):
        src = (i + 16 - di) % 16
        remote(
            disp.at[pl.ds(pl.multiple_of(src * 16, 16), 16), :],
            slots.at[j, pl.ds(pl.multiple_of(src * 16, 16), 16), :],
            d_ss.at[di], d_rs.at[di], (src, j),
        ).wait_recv()
    marks = slots[j, :, 512:640].astype(F32)
    left = jnp.sum(marks * wrow[0:1, :], axis=1, keepdims=True)
    marks = jnp.where(
        iota((256, 128), 1) == 80, jnp.where(left > 0.5, 0.0, 1.0), marks
    )
    slots[j, :, 512:640] = marks.astype(BF16)

    def g_copy(dx):
        return remote(
            slots.at[j], slots.at[j], g_ss.at[dx], g_rs.at[j], (i, 2 * ((x + dx) % 4) + c)
        )

    def g_sib(block, k):
        return remote(slots.at[block], slots.at[block], g_ss.at[k], g_rs.at[block], (i, sib))

    for dx in (2, 1, 3):
        g_copy(dx).start()
    g_sib(j, 0).start()

    @pl.loop(6, 16)
    def _(r):
        cache_part(r)

    def slot_part(block):
        @pl.loop(0, 2)
        def _(t):
            rows = pl.ds(pl.multiple_of(t * 256, 256), 256)
            s = nt(qs[rows, :], slots[block])
            old = m_s[rows, 0:1]
            m = jnp.maximum(old, jnp.max(s, axis=1, keepdims=True))
            keep = jnp.exp2((old - m) * unit)
            e = jnp.exp2((s - m) * unit)
            l_s[rows, :] = l_s[rows, :] * keep + jnp.sum(e, axis=1, keepdims=True)
            acc[rows, :] = acc[rows, :] * keep + nn(e.astype(BF16), slots[block, :, 0:512])
            m_s[rows, :] = jnp.broadcast_to(m, (256, 128))

    def g_wait(block):
        remote(slots.at[block], slots.at[block], g_ss.at[0], g_rs.at[block], (i, sib)).wait_recv()

    slot_part(j)
    g_wait(sib)
    slot_part(sib)
    for k, dx in enumerate((1, 3, 2)):
        block = 2 * ((x + dx) % 4) + c
        g_wait(block)
        g_sib(block, 4 + k).start()
        slot_part(block)
    for dx in (1, 3, 2):
        block = 2 * ((x + dx) % 4) + 1 - c
        g_wait(block)
        slot_part(block)

    @pl.loop(0, 2)
    def _(t):
        rows = pl.ds(pl.multiple_of(t * 256, 256), 256)
        ob[rows, :] = (acc[rows, :] * (1.0 / l_s[rows, 0:1])).astype(BF16)

    @pl.loop(0, 2)
    def _(t):
        n = iota((256, 512), 0) + t * 256
        want = (n & 15) * 32 + (n >> 5) * 2 + ((n >> 4) & 1)
        rows = pl.ds(pl.multiple_of(t * 256, 256), 256)
        op[rows, :] = nn(one_hot(iota((256, 512), 1) == want), ob[...]).astype(BF16)

    c_uv.wait()
    c_wo.wait()

    def o_dev(dz, dy):
        return ((z + dz) % 4) * 4 + (y + dy) % 4

    def h_copy(half, piece, k, to):
        return remote(
            hog.at[half, piece], hog.at[half, piece], h_ss.at[half, k], h_rs.at[half, piece],
            (to, j),
        )

    def h_wait(half, piece):
        remote(
            hog.at[half, piece], hog.at[half, piece], h_ss.at[half, 0], h_rs.at[half, piece],
            (i, sib),
        ).wait_recv()

    def near(half, d):
        return o_dev(0, d) if half == 0 else o_dev(d, 0)

    def far(half, d):
        return o_dev(d, 0) if half == 0 else o_dev(0, d)

    sent = []
    for half in range(2):
        for h in range(8):
            hog[half, i, :, h * 128 : (h + 1) * 128] = nn(
                op[(half * 8 + h) * 32 : (half * 8 + h + 1) * 32, :], uv[half * 8 + h]
            ).astype(BF16)
        for k, d in enumerate((2, 1, 3)):
            cp = h_copy(half, i, k, near(half, d))
            cp.start()
            sent.append(cp)
        for k, d in enumerate((2, 1, 3)):
            cp = h_copy(half, i, 3 + k, far(half, d))
            cp.start()
            sent.append(cp)
    for q, e in enumerate((1, 3, 2)):
        for half in range(2):
            piece = near(half, e)
            h_wait(half, piece)
            for k, d in enumerate((2, 1, 3)):
                cp = h_copy(half, piece, 6 + 3 * q + k, far(half, d))
                cp.start()
                sent.append(cp)

    def o_copy(to):
        return remote(osend.at[to], orecv.at[j], o_ss.at[to], o_rs.at[j], (i, to))

    for dz in (0, 1, 3, 2):
        row = (z + dz) % 4
        for dy in range(4):
            piece = o_dev(dz, dy)
            if dz != 0:
                h_wait(0, piece)
            if dy != 0:
                h_wait(1, piece)
        four = pl.ds(row * 4, 4)
        res = nt(hog[0, four].reshape(128, 1024), wo[:, 0:1024])
        res = res + nt(hog[1, four].reshape(128, 1024), wo[:, 1024:2048])
        for k in range(2):
            to = row * 2 + k
            osend[to, :, 0:448] = res[k * 64 : (k + 1) * 64, :].astype(BF16)

            @pl.when(to != j)
            def _():
                o_copy(to).start()

    total = osend[j, :, 0:448].astype(F32)
    for dj in range(1, 8):
        src = (j + dj) % 8
        remote(osend.at[src], orecv.at[src], o_ss.at[src], o_rs.at[src], (i, src)).wait_recv()
        total = total + orecv[src, :, 0:448].astype(F32)
    total = total.astype(BF16)
    for o in range(2):
        for s in range(2):
            out[s, o * 16 : (o + 1) * 16, :] = total[o * 32 + s * 16 : o * 32 + s * 16 + 16, :]

    for di in range(1, 16):
        t_copy(di).wait_send()
        d_copy(di).wait_send()
    np_pair.wait_send()
    np_swap.wait_send()
    for dx in range(4):
        p_copy(dx).wait_send()
    for dx in range(1, 4):
        npx_copy(dx).wait_send()
        x_copy(dx).wait_send()
        g_copy(dx).wait_send()
    g_sib(j, 0).wait_send()
    for k, dx in enumerate((1, 3, 2)):
        g_sib(2 * ((x + dx) % 4) + c, 4 + k).wait_send()
    for cp in sent:
        cp.wait_send()
    for dj in range(1, 8):
        o_copy((j + dj) % 8).wait_send()


def local(
    prompt_hidden, owner, offsets, cache, lengths, new_hidden, w_down,
    gain_q, gain_kv, w_uq, w_uk, w_uv, w_out,
):
    half = ROPE // 2
    inverse = 10000.0 ** (-jnp.arange(half, dtype=F32) / half)
    angles = (offsets % 1024).astype(F32)[:, None] * inverse
    cos, sin = jnp.cos(angles), jnp.sin(angles)
    ctab = jnp.concatenate([cos, cos, -sin, sin], axis=1)
    lane = jnp.arange(128, dtype=I32)[None, :]
    off = offsets[:, None]
    place = off % 1024
    ex = (
        jnp.where(lane == 64 + off // 1024, 1, 0)
        + jnp.where(lane == 81, place // 128, 0)
        + jnp.where(lane == 82, place % 128, 0)
    ).astype(BF16)
    positions = (lengths[None, :] + jnp.arange(2, dtype=I32)[:, None]).reshape(32)
    angles = positions.astype(F32)[:, None] * inverse
    cos, sin = jnp.cos(angles), jnp.sin(angles)
    ntab = jnp.stack(
        [
            jnp.concatenate([cos, cos, -sin, sin], axis=1),
            jnp.concatenate([cos, cos, cos, cos], axis=1),
            jnp.concatenate([-sin, sin, -sin, sin], axis=1),
        ]
    )
    row = jnp.arange(128, dtype=I32)[:, None]
    nex = jnp.where(
        row < 32,
        jnp.where(lane == 64 + row % 16, 1.0, 0.0) + jnp.where(lane == 83, row // 16, 0),
        jnp.where(lane == 80, 1.0, 0.0),
    ).astype(F32)
    row = row[:32]
    other = (lane >= 64) & (lane < 80) & (lane != 64 + row % 16)
    qex = jnp.where(other | (lane == 80) | ((lane == 83) & (row < 16)), HIDE, 0.0).astype(F32)
    cell = jnp.arange(16384, dtype=I32).reshape(16, 1024)
    vis = jnp.where((cell % 1024) < lengths[:, None], 1.0, 0.0).astype(F32).reshape(128, 128)
    wrow = jnp.concatenate(
        [jnp.zeros((64,), F32), lengths.astype(F32), jnp.array([0.0, -128.0, -1.0], F32),
         jnp.zeros((45,), F32)]
    )
    wrow = jnp.broadcast_to(wrow[None, :], (8, 128))

    vm = pl.BlockSpec(memory_space=pltpu.VMEM)
    hb = pl.BlockSpec(memory_space=pl.ANY)
    V = pltpu.VMEM
    S = pltpu.SemaphoreType.DMA
    scratch = [
        V((1024, 896), BF16), V((2112, 896), BF16), V((1536, 3072), BF16), V((16, 128, 512), BF16),
        V((16, 576, 1024), BF16), V((16, 512, 128), BF16), V((448, 2048), BF16), S((6,)), S((16,)),
        V((16, 128), I32), V((16, 8, 128), F32), V((16, 8, 128), F32), S((16,)), S((16,)),
        V((2, 32, 1152), BF16), V((32, 1152), BF16), V((32, 1152), BF16), V((4, 32, 1152), BF16),
        V((2, 32, 1152), BF16), S((5,)), S((5,)),
        V((128, 896), BF16), V((1024, 640), BF16), V((4, 128, 640), BF16), V((4, 128, 640), BF16),
        V((4, 128, 640), BF16), V((4, 128, 640), BF16), V((128, 640), F32),
        S((4,)), S((4,)), S((4,)), S((4,)),
        V((256, 640), BF16), V((8, 256, 640), BF16), S((16,)), S((16,)), S((8,)), S((8,)),
        V((32, 1536), BF16), V((512, 640), BF16), V((512, 640), BF16), V((128, 640), BF16),
        V((128, 128), F32), V((512, 512), F32), V((512, 128), F32), V((512, 128), F32),
        V((512, 512), BF16), V((512, 512), BF16),
        V((2, 16, 32, 1024), BF16), S((2, 15)), S((2, 16)),
        V((8, 64, 512), BF16), V((8, 64, 512), BF16), S((8,)), S((8,)),
    ]
    return pl.pallas_call(
        kernel,
        out_shape=jax.ShapeDtypeStruct((2, 32, 448), BF16),
        in_specs=[vm] * 12 + [hb] * 7,
        out_specs=vm,
        scratch_shapes=scratch,
        compiler_params=pltpu.CompilerParams(
            collective_id=0, has_side_effects=True, vmem_limit_bytes=60 * 1024 * 1024
        ),
    )(
        owner.reshape(8, 128), offsets.reshape(8, 128), ctab, ex, ntab, nex, qex, vis, wrow,
        gain_q.astype(F32).reshape(1, QRANK), gain_kv.astype(F32).reshape(1, LATENT),
        new_hidden.reshape(32, 896),
        prompt_hidden, w_down.T, w_uq, w_uk, jnp.swapaxes(cache, 1, 2), w_uv, w_out.T,
    )


def solution(mesh):
    in_specs = (
        P("seq", "head"), P("seq", None), P("seq"), P("seq", None, None), P("seq"),
        P(None, "seq", "head"), P("head", None), P(), P(), P(None, "head"),
        P("head", None, None), P("head", None, None), P("head", "seq"),
    )
    return jax.shard_map(
        local, mesh=mesh, in_specs=in_specs, out_specs=P(None, "head", "seq"), check_vma=False
    )
```

```python
import functools

import jax
import jax.numpy as jnp
from jax import lax
from jax.experimental import pallas as pl
from jax.experimental.pallas import tpu as pltpu
from jax.sharding import PartitionSpec as P

F32 = jnp.float32
BF16 = jnp.bfloat16
I32 = jnp.int32
MESH = pl.DeviceIdType.MESH
QRANK = 1536
LATENT = 512
ROPE = 64
NOPE = 128
VDIM = 128
HIDE = -1e30
LOG2E = 1.4426950408889634
LOG2_BASE = 13.287712379549449


def nt(a, b):
    return lax.dot_general(a, b, (((1,), (1,)), ((), ())), preferred_element_type=F32)


def nn(a, b):
    return jnp.dot(a, b, preferred_element_type=F32)


def iota(shape, dim):
    return lax.broadcasted_iota(I32, shape, dim)


def one_hot(cond):
    return jnp.where(cond, 1.0, 0.0).astype(BF16)


def turn_rate(lane):
    return jnp.exp2((lane & 31).astype(F32) * (-LOG2_BASE / (ROPE // 2)))


def turned(v):
    inner = (iota(v.shape, 1) & 63) < 32
    return jnp.where(inner, pltpu.roll(v, 96, 1), pltpu.roll(v, 32, 1))


def kernel(
    lens, own_r, off_r, gain_q, gain_kv, newh,
    hid_h, wd_h, uq_h, uk_h, cache_h, uv_h, wo_h,
    out,
    hid, wd, uq, uk, kc, uv, wo, lsem, ksem,
    rs, feat, tsend, trecv, ts_sem, tr_sem,
    npp, npair, npx, npxr, npfin, np_ss, np_rs, ntab,
    part, ps, pr, xs, xr, mine, p_ss, p_rs, x_ss, x_rs,
    disp, slots, d_ss, d_rs, g_ss, g_rs,
    qls, ql, qs, newk, biasm, acc, m_s, l_s, ob, op,
    hog, h_ss, h_rs, ores, opair, opin, op_ss, op_rs, osend, orecv, o_ss, o_rs,
):
    i = lax.axis_index("seq")
    j = lax.axis_index("head")
    x = j // 2
    c = j % 2
    z = i // 4
    y = i % 4
    sib = 2 * x + (1 - c)

    def load(src, dst, sem):
        cp = pltpu.make_async_copy(src, dst, sem)
        cp.start()
        return cp

    def remote(src, dst, ss, rr, dev):
        return pltpu.make_async_remote_copy(
            src_ref=src, dst_ref=dst, send_sem=ss, recv_sem=rr,
            device_id=dev, device_id_type=MESH,
        )

    barrier = pltpu.get_barrier_semaphore()
    for dj in range(1, 8):
        pl.semaphore_signal(barrier, inc=1, device_id=(i, (j + dj) % 8), device_id_type=MESH)
    for di in range(1, 16):
        pl.semaphore_signal(barrier, inc=1, device_id=((i + di) % 16, j), device_id_type=MESH)

    c_wd = load(wd_h, wd, lsem.at[0])
    c_hid = load(hid_h, hid, lsem.at[1])

    sub128 = iota((128, 128), 0)
    lane128 = iota((128, 128), 1)
    sub16 = iota((16, 128), 0)
    hot = jnp.concatenate(
        [jnp.where(sub16 == own_r[b : b + 1, :], 1.0, 0.0) for b in range(8)], axis=0
    )
    hot_b = hot.astype(BF16)
    ahead = nn(hot_b, one_hot(sub128 < lane128))
    count = nn(hot_b, jnp.ones((128, 128), BF16)).astype(BF16)
    before = ((lane128 & 15) < (sub128 & 15)) | (
        ((lane128 & 15) == (sub128 & 15)) & ((lane128 >> 4) < (sub128 >> 4))
    )
    ahead = ahead + nn(one_hot(before), count)
    ends = nn(one_hot((iota((16, 128), 1) & 15) <= sub16), count)
    place = jnp.sum((hot * ahead).reshape(8, 16, 128), axis=1).astype(I32)
    dev = place & 7
    at = place >> 3
    rs[0:8, :] = dev * 128 + at
    key = dev * 16 + (at & 15)
    mine_at = rs[0:8, :] - j * 128
    off = off_r[...]
    digits, keys, marks, picks = [], [], [], []
    sub32 = iota((32, 128), 0)
    for b in range(8):
        one = slice(b, b + 1)
        high, low = (off[one] >> 7).astype(F32), (off[one] & 127).astype(F32)
        hb = hot[b * 16 : b * 16 + 16]
        digits.append(jnp.concatenate([hb * high, hb * low, hb], axis=0).astype(BF16))
        keys.append(one_hot(sub128 == key[one]))
        mark = jnp.where(sub32 == (off[one] >> 10), 1.0, 0.0)
        mark = jnp.where(sub32 == 17, ((off[one] >> 7) & 7).astype(F32), mark)
        mark = jnp.where(sub32 == 18, low, mark)
        marks.append(
            jnp.concatenate([jnp.zeros((64, 128), F32), mark, jnp.zeros((32, 128), F32)], axis=0)
            .astype(BF16)
        )
        picks.append(one_hot(sub128 == mine_at[one]))
    table = nt(jnp.concatenate(digits, axis=1), jnp.concatenate(keys, axis=1))
    feat[...] = nt(jnp.concatenate(picks, axis=1), jnp.concatenate(marks, axis=1))
    cells = jnp.where(table[32:48] > 0.5, table[0:16] * 128.0 + table[16:32], -1.0)
    for o in range(16):
        tsend[o] = jnp.broadcast_to(cells[o : o + 1, :], (8, 128))
    row_place = (iota((16, 128), 1) * 8 + j).astype(F32)
    owner_at = jnp.sum(
        jnp.where(row_place >= ends, 1.0, 0.0), axis=0, keepdims=True
    ).astype(I32)
    slot_at = owner_at * 16 + (iota((1, 128), 1) & 15)
    rs[8:9, :] = slot_at
    request = iota((32, 128), 0) & 15
    position = iota((32, 128), 0) >> 4
    for r in range(16):
        position = position + jnp.where(request == r, lens[r], 0)
    lane32 = iota((32, 128), 1)
    angle = position.astype(F32) * turn_rate(lane32)
    ntab[0] = jnp.cos(angle)
    ntab[1] = jnp.where((lane32 & 63) < 32, -1.0, 1.0) * jnp.sin(angle)

    c_wd.wait()
    c_uq = load(uq_h, uq, lsem.at[2])
    c_uk = load(uk_h, uk, lsem.at[3])
    npp[0] = nt(newh[...], wd[0:1152, :]).astype(BF16)
    npp[1, :, 0:896] = nt(newh[...], wd[1152:2048, :]).astype(BF16)
    tail = nt(newh[...], wd[2048:2112, :])
    npp[1, :, 896:1024] = jnp.concatenate([tail, tail], axis=1).astype(BF16)
    npp[1, :, 1024:1152] = jnp.zeros((32, 128), BF16)
    c_hid.wait()

    def k_copy(r):
        return pltpu.make_async_copy(cache_h.at[r], kc.at[r], ksem.at[r])

    @pl.loop(0, 16)
    def _(r):
        k_copy(r).start()

    c_uv = load(uv_h, uv, lsem.at[4])
    c_wo = load(wo_h, wo, lsem.at[5])
    def project(t):
        rows = pl.ds(t * 512, 512)
        h = hid[rows, :]
        part[rows, 0:512] = nt(h, wd[1536:2048, :]).astype(BF16)
        u = nt(h, wd[2048:2112, :])
        part[rows, 512:640] = jnp.concatenate([u, u], axis=1).astype(BF16)

    def npx_copy(dx):
        return remote(
            npx, npxr.at[dx], np_ss.at[dx], np_rs.at[dx], (i, 2 * ((x + dx) % 4) + c)
        )

    project(0)
    project(1)

    def permuted(first, second):
        ids = rs[0:8, :]
        top = [one_hot(sub128 == ids[b : b + 1, :] - first * 128) for b in range(8)]
        low = [one_hot(sub128 == ids[b : b + 1, :] - second * 128) for b in range(8)]
        pick = jnp.concatenate(
            [jnp.concatenate(top, axis=1), jnp.concatenate(low, axis=1)], axis=0
        )
        return nn(pick, part[...])

    def p_copy(dx):
        return remote(ps.at[dx], pr.at[dx], p_ss.at[dx], p_rs.at[dx], (i, sib))

    def via_copy(k):
        return remote(
            xs.at[2, pl.ds(64 * k, 64), :], xr.at[2, pl.ds(64 * k, 64), :],
            x_ss.at[k], x_rs.at[k], (i, 2 * ((x + 1 + 2 * k) % 4) + c),
        )

    def x_copy(dx, k):
        rows = pl.ds(64 * k, 64)
        return remote(
            xs.at[dx, rows, :], xr.at[dx, rows, :], x_ss.at[2 * dx + k], x_rs.at[2 * dx + k],
            (i, 2 * ((x + dx) % 4) + c),
        )

    for first, second in ((2, 1), (3, 0)):
        both = permuted(2 * ((x + first) % 4) + 1 - c, 2 * ((x + second) % 4) + 1 - c)
        ps[first] = both[0:128].astype(BF16)
        ps[second] = both[128:256].astype(BF16)

    pl.semaphore_wait(barrier, 22)
    np_pair = remote(npp.at[1 - c], npair, np_ss.at[0], np_rs.at[0], (i, sib))
    np_pair.start()
    for dx in (2, 1, 3, 0):
        p_copy(dx).start()

    def t_copy(di):
        to = (i + di) % 16
        return remote(tsend.at[to], trecv.at[i], ts_sem.at[di], tr_sem.at[di], (to, j))

    for di in range(1, 16):
        t_copy(di).start()
    both = permuted(2 * ((x + 2) % 4) + c, 2 * ((x + 1) % 4) + c)
    np_pair.wait_recv()
    npx[...] = (npp[c].astype(F32) + npair[...].astype(F32)).astype(BF16)
    for dx in (2, 1, 3):
        npx_copy(dx).start()
    p_copy(2).wait_recv()
    xs[2] = (both[0:128] + pr[2].astype(F32)).astype(BF16)
    via_copy(0).start()
    via_copy(1).start()
    p_copy(1).wait_recv()
    up = both[128:256] + pr[1].astype(F32)
    xs[1, 64:128, :] = up[64:128].astype(BF16)
    x_copy(1, 1).start()
    both = permuted(2 * ((x + 3) % 4) + c, 2 * x + c)
    p_copy(3).wait_recv()
    down = both[0:128] + pr[3].astype(F32)
    xs[3, 0:64, :] = down[0:64].astype(BF16)
    x_copy(3, 0).start()
    p_copy(0).wait_recv()
    mine[...] = both[128:256] + pr[0].astype(F32)

    total = npx[...].astype(F32)
    for dx in (1, 3, 2):
        npx_copy(dx).wait_recv()
        total = total + npxr[dx].astype(F32)
    npfin[c] = total.astype(BF16)
    np_swap = remote(npfin.at[c], npfin.at[c], np_ss.at[4], np_rs.at[4], (i, sib))
    np_swap.start()
    via_copy(0).wait_recv()
    xs[1, 0:64, :] = (up[0:64] + xr[2, 0:64, :].astype(F32)).astype(BF16)
    x_copy(1, 0).start()
    via_copy(1).wait_recv()
    xs[3, 64:128, :] = (down[64:128] + xr[2, 64:128, :].astype(F32)).astype(BF16)
    x_copy(3, 1).start()
    np_swap_in = remote(npfin.at[1 - c], npfin.at[1 - c], np_ss.at[4], np_rs.at[4], (i, sib))
    np_swap_in.wait_recv()

    unit = LOG2E / (NOPE + ROPE) ** 0.5
    low32 = iota((32, 128), 1) < 64
    q_in = jnp.concatenate([npfin[0], npfin[1, :, 0:384]], axis=1).astype(F32)
    q_in = q_in * lax.rsqrt(jnp.mean(q_in * q_in, axis=1, keepdims=True) + 1e-6) * gain_q[...].astype(F32).reshape(1, QRANK)
    qls[...] = q_in.astype(BF16)
    k_in = npfin[1, :, 384:896].astype(F32)
    k_in = k_in * lax.rsqrt(jnp.mean(k_in * k_in, axis=1, keepdims=True) + 1e-6) * gain_kv[...].astype(F32).reshape(1, LATENT)
    newk[0:32, 0:512] = k_in.astype(BF16)
    newk[32:128, 0:512] = jnp.zeros((96, 512), BF16)
    u = npfin[1, :, 896:1024].astype(F32)
    u = u * ntab[0] + turned(u) * ntab[1]
    row32 = iota((32, 128), 0)
    own_lane = lane32 == 64 + (row32 & 15)
    late = (lane32 == 83) & (row32 >= 16)
    u = jnp.where(low32, u, jnp.where(own_lane | late, 1.0, 0.0))
    newk[0:32, 512:640] = u.astype(BF16)
    newk[32:128, 512:640] = one_hot(iota((96, 128), 1) == 80)
    other = (lane32 >= 64) & (lane32 < 81) & jnp.logical_not(own_lane)
    qex = jnp.where(other | ((lane32 == 83) & (row32 < 16)), HIDE, 0.0)

    c_uq.wait()
    c_uk.wait()

    def two_heads(p):
        q = nn(qls[...], uq[:, pl.ds(pl.multiple_of(p * 384, 384), 384)])
        t0, t1, t2 = q[:, 0:128], q[:, 128:256], q[:, 256:384]
        odd = jnp.where(low32, pltpu.roll(t1, 64, 1), pltpu.roll(t2, 64, 1))
        rope = jnp.where(low32, t1, t2)
        rope = rope * ntab[0] + turned(rope) * ntab[1]
        for s, (nope, rot) in enumerate(((t0, rope), (odd, pltpu.roll(rope, 64, 1)))):
            rows = pl.ds(pl.multiple_of(p * 64 + s * 32, 32), 32)
            ql[rows, 0:512] = (nn(nope.astype(BF16), uk[2 * p + s]) * unit).astype(BF16)
            ql[rows, 512:640] = jnp.where(low32, rot * unit, qex).astype(BF16)

    @pl.loop(0, 4)
    def _(p):
        two_heads(2 * p)
        two_heads(2 * p + 1)

    @pl.loop(0, 2)
    def _(t):
        n = iota((256, 512), 0) + t * 256
        want = ((n & 31) >> 1) * 32 + (n & 1) * 16 + (n >> 5)
        rows = pl.ds(pl.multiple_of(t * 256, 256), 256)
        qs[rows, :] = nn(one_hot(iota((256, 512), 1) == want), ql[...]).astype(BF16)

    total = mine[...]
    for dx in (1, 3):
        x_copy(dx, 0).wait_recv()
        x_copy(dx, 1).wait_recv()
        total = total + xr[dx].astype(F32)
    lat = total[:, 0:512]
    lat = lat * lax.rsqrt(jnp.mean(lat * lat, axis=1, keepdims=True) + 1e-6) * gain_kv[...].astype(F32).reshape(1, LATENT)
    tail = total[:, 512:640]
    marks = feat[...]
    at = jnp.where(lane128 == 81, 128.0, jnp.where(lane128 == 82, 1.0, 0.0))
    at = jnp.sum(marks * at, axis=1, keepdims=True)
    angle = at * turn_rate(lane128)
    sign = jnp.where((lane128 & 63) < 32, -1.0, 1.0)
    tail = tail * jnp.cos(angle) + turned(tail) * (sign * jnp.sin(angle))
    tail = jnp.where(lane128 < 64, tail, marks)
    rows_b = jnp.concatenate([lat, tail], axis=1).astype(BF16)
    spread = one_hot(iota((256, 128), 0) == rs[8:9, :])
    disp[...] = nn(spread, rows_b).astype(BF16)

    def d_copy(di):
        to = (i + di) % 16
        return remote(
            disp.at[pl.ds(pl.multiple_of(to * 16, 16), 16), :],
            slots.at[j, pl.ds(pl.multiple_of(i * 16, 16), 16), :],
            d_ss.at[di], d_rs.at[di], (to, j),
        )

    for di in range(1, 16):
        d_copy(di).start()
    at_me = pl.ds(pl.multiple_of(i * 16, 16), 16)
    slots[j, at_me, :] = disp[at_me, :]

    at_src = tsend[i]
    trecv[i] = at_src
    for di in range(1, 16):
        src = (i + 16 - di) % 16
        remote(tsend.at[src], trecv.at[src], ts_sem.at[di], tr_sem.at[di], (src, j)).wait_recv()

    tall, wide = [], []
    for s in range(16):
        cell = trecv[s, 0:1, :].astype(I32)
        tall.append(one_hot(sub128 == (cell >> 7)))
        wide.append(one_hot(sub128 == (cell & 127)))
    taken = nt(jnp.concatenate(tall, axis=1), jnp.concatenate(wide, axis=1))
    length = jnp.zeros((128, 128), I32)
    weigh = jnp.where(iota((8, 128), 1) == 81, -128.0, 0.0)
    weigh = jnp.where(iota((8, 128), 1) == 82, -1.0, weigh)
    for r in range(16):
        length = length + jnp.where((sub128 >> 3) == r, lens[r], 0)
        weigh = weigh + jnp.where(iota((8, 128), 1) == 64 + r, lens[r], 0).astype(F32)
    seen = (sub128 & 7) * 128 + lane128 < length
    biasm[...] = jnp.where((taken < 0.5) & seen, 0.0, HIDE)

    def cache_part(r):
        rows = pl.ds(pl.multiple_of(r * 32, 32), 32)
        s = nn(qs[rows, 0:576], kc[r])
        b8 = biasm[pl.ds(pl.multiple_of(r * 8, 8), 8), :]
        s = [s[:, g * 128 : (g + 1) * 128] + b8[g : g + 1, :] for g in range(8)]
        s.append(nt(qs[rows, :], newk[...]))
        top = jnp.max(functools.reduce(jnp.maximum, s), axis=1, keepdims=True)
        m = jnp.broadcast_to(top, (32, 128))
        e = [jnp.exp2(v - m) for v in s]
        m_s[rows, :] = m
        l_s[rows, :] = functools.reduce(jnp.add, e)
        e = [v.astype(BF16) for v in e]
        acc[rows, :] = nt(jnp.concatenate(e[0:8], axis=1), kc[r, 0:512, :]) + nn(
            e[8], newk[:, 0:512]
        )

    def cache_four(t):
        for r in range(4):
            k_copy(4 * t + r).wait()
        for r in range(4):
            cache_part(4 * t + r)

    @pl.loop(0, 1)
    def _(t):
        cache_four(t)

    for di in range(1, 16):
        src = (i + 16 - di) % 16
        remote(
            disp.at[pl.ds(pl.multiple_of(src * 16, 16), 16), :],
            slots.at[j, pl.ds(pl.multiple_of(src * 16, 16), 16), :],
            d_ss.at[di], d_rs.at[di], (src, j),
        ).wait_recv()
    marks = slots[j, :, 512:640].astype(F32)
    left = jnp.sum(marks * weigh[0:1, :], axis=1, keepdims=True)
    marks = jnp.where(
        iota((256, 128), 1) == 80, jnp.where(left > 0.5, 0.0, 1.0), marks
    )
    slots[j, :, 512:640] = marks.astype(BF16)

    def g_half(block, k):
        return slots.at[block, pl.ds(128 * k, 128), :]

    def g_copy(block, k, ss, to):
        return remote(
            g_half(block, k), g_half(block, k), g_ss.at[ss], g_rs.at[block, k], (i, to)
        )

    def g_wait(block, k):
        g_copy(block, k, 0, sib).wait_recv()

    above, below, across = 2 * ((x + 1) % 4), 2 * ((x + 3) % 4), 2 * ((x + 2) % 4)
    g_sent = []

    def g_send(block, k, to):
        cp = g_copy(block, k, len(g_sent), to)
        cp.start()
        g_sent.append(cp)

    g_send(j, 0, above + c)
    g_send(j, 1, below + c)
    g_send(j, 1, above + c)
    g_send(j, 0, below + c)
    g_send(j, 0, sib)
    g_send(j, 1, sib)

    def slot_part(first, second):
        q = qs[...]
        blocks = (first, second)
        s = [nt(q, slots[b]) for b in blocks]
        s = [v[:, g * 128 : (g + 1) * 128] for v in s for g in range(2)]
        old = m_s[...]
        top = jnp.max(functools.reduce(jnp.maximum, s), axis=1, keepdims=True)
        m = jnp.maximum(old, jnp.broadcast_to(top, (512, 128)))
        keep = jnp.exp2(old - m)
        e = [jnp.exp2(v - m) for v in s]
        m_s[...] = m
        l_s[...] = l_s[...] * keep + functools.reduce(jnp.add, e)
        e = [v.astype(BF16) for v in e]
        val = nn(jnp.concatenate(e[0:2], axis=1), slots[first, :, 0:512])
        val = val + nn(jnp.concatenate(e[2:4], axis=1), slots[second, :, 0:512])
        acc[...] = acc[...] * jnp.concatenate([keep] * 4, axis=1) + val

    @pl.loop(1, 2)
    def _(t):
        cache_four(t)

    g_wait(below + c, 0)
    g_send(below + c, 0, above + c)
    g_wait(above + c, 1)
    g_send(above + c, 1, below + c)
    g_send(below + c, 0, sib)
    g_send(above + c, 1, sib)

    @pl.loop(2, 3)
    def _(t):
        cache_four(t)

    g_wait(below + c, 1)
    g_send(below + c, 1, sib)
    g_wait(above + c, 0)
    g_send(above + c, 0, sib)

    @pl.loop(3, 4)
    def _(t):
        cache_four(t)

    @pl.loop(0, 2)
    def _(t):
        chip = 2 * ((x + 3 * t) % 4)
        for k in range(2):
            g_wait(chip + 1 - c, k)
        slot_part(chip + c, chip + 1 - c)

    g_wait(across + c, 0)
    g_send(across + c, 0, sib)
    g_wait(across + c, 1)
    g_send(across + c, 1, sib)

    @pl.loop(0, 2)
    def _(t):
        chip = 2 * ((x + 1 + t) % 4)
        for k in range(2):
            g_wait(chip + 1 - c, k)
        slot_part(chip + c, chip + 1 - c)

    @pl.loop(0, 2)
    def _(t):
        rows = pl.ds(pl.multiple_of(t * 256, 256), 256)
        ob[rows, :] = (
            acc[rows, :] * (1.0 / jnp.sum(l_s[rows, :], axis=1, keepdims=True))
        ).astype(BF16)

    @pl.loop(0, 2)
    def _(t):
        n = iota((256, 512), 0) + t * 256
        want = (n & 15) * 32 + (n >> 5) * 2 + ((n >> 4) & 1)
        rows = pl.ds(pl.multiple_of(t * 256, 256), 256)
        op[rows, :] = nn(one_hot(iota((256, 512), 1) == want), ob[...]).astype(BF16)

    c_uv.wait()
    c_wo.wait()

    def o_dev(dz, dy):
        return ((z + dz) % 4) * 4 + (y + dy) % 4

    def near(half, d):
        return o_dev(0, d) if half == 0 else o_dev(d, 0)

    def far(half, d):
        return o_dev(d, 0) if half == 0 else o_dev(0, d)

    def cross(half, n, f):
        return o_dev(f, n) if half == 0 else o_dev(n, f)

    h_sent = []

    def h_copy(half, piece, part_at, k, to):
        ref = hog.at[half, piece]
        if part_at is not None:
            ref = hog.at[half, piece, pl.ds(16 * part_at, 16), :]
        return remote(ref, ref, h_ss.at[k], h_rs.at[half, piece, part_at or 0], (to, j))

    def h_send(half, piece, part_at, to):
        cp = h_copy(half, piece, part_at, len(h_sent), to)
        cp.start()
        h_sent.append(cp)

    def h_wait(half, piece, part_at=None):
        h_copy(half, piece, part_at, 0, i).wait_recv()

    halves = range(2)
    for half in halves:
        for h in range(8):
            hog[half, i, :, h * 128 : (h + 1) * 128] = nn(
                op[(half * 8 + h) * 32 : (half * 8 + h + 1) * 32, :], uv[half * 8 + h]
            ).astype(BF16)
        for d in (1, 3):
            h_send(half, i, None, near(half, d))
        for d in (1, 3):
            h_send(half, i, None, far(half, d))

    def pass_on(half, n, f, to):
        piece = cross(half, n, f)
        h_wait(half, piece)
        h_send(half, piece, 0 if (f == 3 or (f == 0 and n == 3)) else 1, to)

    for n in (3, 1):
        for half in halves:
            pass_on(half, n, 0, near(half, 4 - n))
            for d in (1, 3):
                h_send(half, near(half, n), None, far(half, d))
    for f in (3, 1):
        for half in halves:
            pass_on(half, 0, f, far(half, 4 - f))
    for half in halves:
        h_wait(half, near(half, 2), 0)
        h_wait(half, near(half, 2), 1)
        for d in (1, 3):
            h_send(half, near(half, 2), None, far(half, d))
    for n in (3, 1):
        for f in (3, 1):
            for half in halves:
                pass_on(half, n, f, far(half, 4 - f))

    def o_pair(t):
        return remote(opair.at[t], opin.at[t], op_ss.at[t], op_rs.at[t], (i, sib))

    def o_copy(t, to):
        return remote(osend.at[t], orecv.at[x], o_ss.at[t], o_rs.at[x], (i, 2 * to + c))

    def columns(t, row):
        four = pl.ds(row * 4, 4)
        res = nt(hog[0, four].reshape(128, 1024), wo[:, 0:1024])
        res = res + nt(hog[1, four].reshape(128, 1024), wo[:, 1024:2048])
        ores[t, :, 0:448] = res
        opair[t, :, 0:448] = ores[t, pl.ds(pl.multiple_of((1 - c) * 64, 64), 64), 0:448].astype(
            BF16
        )
        o_pair(t).start()

    def onward(t, row):
        o_pair(t).wait_recv()
        own_half = ores[t, pl.ds(pl.multiple_of(c * 64, 64), 64), :]
        osend[t] = (own_half + opin[t].astype(F32)).astype(BF16)

        @pl.when(row != x)
        def _():
            o_copy(t, row).start()

        @pl.when(row == x)
        def _():
            orecv[x] = osend[t]

    order = (0, 3, 1, 2)
    rows_at = [(z + dz) % 4 for dz in order]
    h_wait(1, far(1, 2), 0)
    h_wait(1, far(1, 2), 1)
    columns(0, rows_at[0])
    for t, d in ((1, 3), (2, 1)):
        h_wait(0, cross(0, 2, d))
        h_send(0, cross(0, 2, d), 0 if d == 3 else 1, far(0, 4 - d))
        h_wait(1, cross(1, 2, d))
        h_send(1, cross(1, 2, d), 0 if d == 3 else 1, far(1, 4 - d))
        for k in range(2):
            h_wait(1, cross(1, d, 2), k)
        columns(t, rows_at[t])
        onward(t - 1, rows_at[t - 1])
    for n in range(4):
        for k in range(2):
            h_wait(0, cross(0, n, 2), k)
    for k in range(2):
        h_wait(1, cross(1, 2, 2), k)
    columns(3, rows_at[3])
    onward(2, rows_at[2])
    onward(3, rows_at[3])

    total = jnp.zeros((64, 448), F32)
    for dx in range(1, 4):
        src = (x + dx) % 4
        remote(osend.at[0], orecv.at[src], o_ss.at[0], o_rs.at[src], (i, 2 * src + c)).wait_recv()
    for src in range(4):
        total = total + orecv[src, :, 0:448].astype(F32)
    total = total.astype(BF16)
    for o in range(2):
        for s in range(2):
            out[s, o * 16 : (o + 1) * 16, :] = total[o * 32 + s * 16 : o * 32 + s * 16 + 16, :]

    for di in range(1, 16):
        t_copy(di).wait_send()
        d_copy(di).wait_send()
    np_pair.wait_send()
    np_swap.wait_send()
    for dx in range(4):
        p_copy(dx).wait_send()
    for dx in range(1, 4):
        npx_copy(dx).wait_send()
    for k in range(2):
        x_copy(1, k).wait_send()
        x_copy(3, k).wait_send()
        via_copy(k).wait_send()
    for cp in g_sent + h_sent:
        cp.wait_send()
    for t in range(4):
        o_pair(t).wait_send()

        @pl.when(rows_at[t] != x)
        def _():
            o_copy(t, rows_at[t]).wait_send()


def local(
    prompt_hidden, owner, offsets, cache, lengths, new_hidden, w_down,
    gain_q, gain_kv, w_uq, w_uk, w_uv, w_out,
):
    vm = pl.BlockSpec(memory_space=pltpu.VMEM)
    hb = pl.BlockSpec(memory_space=pl.ANY)
    V = pltpu.VMEM
    S = pltpu.SemaphoreType.DMA
    scratch = [
        V((1024, 896), BF16), V((2112, 896), BF16), V((1536, 3072), BF16), V((16, 128, 512), BF16),
        V((16, 576, 1024), BF16), V((16, 512, 128), BF16), V((448, 2048), BF16), S((6,)), S((16,)),
        V((16, 128), I32), V((128, 128), F32), V((16, 8, 128), F32), V((16, 8, 128), F32), S((16,)), S((16,)),
        V((2, 32, 1152), BF16), V((32, 1152), BF16), V((32, 1152), BF16), V((4, 32, 1152), BF16),
        V((2, 32, 1152), BF16), S((5,)), S((5,)), V((2, 32, 128), F32),
        V((1024, 640), BF16), V((4, 128, 640), BF16), V((4, 128, 640), BF16),
        V((4, 128, 640), BF16), V((4, 128, 640), BF16), V((128, 640), F32),
        S((4,)), S((4,)), S((8,)), S((8,)),
        V((256, 640), BF16), V((8, 256, 640), BF16), S((16,)), S((16,)), S((14,)), S((8, 2)),
        V((32, 1536), BF16), V((512, 640), BF16), V((512, 640), BF16), V((128, 640), BF16),
        V((128, 128), F32), V((512, 512), F32), V((512, 128), F32), V((512, 128), F32),
        V((512, 512), BF16), V((512, 512), BF16),
        V((2, 16, 32, 1024), BF16), S((40,)), S((2, 16, 2)),
        V((4, 128, 512), F32), V((4, 64, 512), BF16), V((4, 64, 512), BF16), S((4,)), S((4,)),
        V((4, 64, 512), BF16), V((4, 64, 512), BF16), S((4,)), S((4,)),
    ]
    return pl.pallas_call(
        kernel,
        out_shape=jax.ShapeDtypeStruct((2, 32, 448), BF16),
        in_specs=[pl.BlockSpec(memory_space=pltpu.SMEM)] + [vm] * 5 + [hb] * 7,
        out_specs=vm,
        scratch_shapes=scratch,
        compiler_params=pltpu.CompilerParams(
            collective_id=0, has_side_effects=True, vmem_limit_bytes=60 * 1024 * 1024
        ),
    )(
        lengths, owner.reshape(8, 128), offsets.reshape(8, 128),
        gain_q, gain_kv,
        new_hidden.reshape(32, 896),
        prompt_hidden, w_down.T, w_uq, w_uk, jnp.swapaxes(cache, 1, 2), w_uv, w_out.T,
    )


def solution(mesh):
    in_specs = (
        P("seq", "head"), P("seq", None), P("seq"), P("seq", None, None), P("seq"),
        P(None, "seq", "head"), P("head", None), P(), P(), P(None, "head"),
        P("head", None, None), P("head", None, None), P("head", "seq"),
    )
    return jax.shard_map(
        local, mesh=mesh, in_specs=in_specs, out_specs=P(None, "head", "seq"), check_vma=False
    )
```

```python
import functools

import jax
import jax.numpy as jnp
from jax import lax
from jax.experimental import pallas as pl
from jax.experimental.pallas import tpu as pltpu
from jax.sharding import PartitionSpec as P

F32 = jnp.float32
BF16 = jnp.bfloat16
I32 = jnp.int32
MESH = pl.DeviceIdType.MESH
QRANK = 1536
LATENT = 512
ROPE = 64
NOPE = 128
VDIM = 128
HIDE = -1e30
LOG2E = 1.4426950408889634
LOG2_BASE = 13.287712379549449


def nt(a, b):
    return lax.dot_general(a, b, (((1,), (1,)), ((), ())), preferred_element_type=F32)


def nn(a, b):
    return jnp.dot(a, b, preferred_element_type=F32)


def iota(shape, dim):
    return lax.broadcasted_iota(I32, shape, dim)


def one_hot(cond):
    return jnp.where(cond, 1.0, 0.0).astype(BF16)


def turn_rate(lane):
    return jnp.exp2((lane & 31).astype(F32) * (-LOG2_BASE / (ROPE // 2)))


def turned(v):
    inner = (iota(v.shape, 1) & 63) < 32
    return jnp.where(inner, pltpu.roll(v, 96, 1), pltpu.roll(v, 32, 1))


def kernel(
    lens, own_r, off_r, gain_q, gain_kv, newh,
    hid_h, wd_h, uq_h, uk_h, cache_h, uv_h, wo_h,
    out,
    hid, wd, uq, uk, kc, uv, wo, lsem, ksem,
    rs, feat, tsend, trecv, ts_sem, tr_sem,
    npp, npair, npx, npxr, npfin, np_ss, np_rs, ntab,
    part, ps, pr, xs, xr, mine, p_ss, p_rs, x_ss, x_rs,
    disp, slots, d_ss, d_rs, g_ss, g_rs,
    qls, ql, qs, newk, snew, enew, biasm, acc, m_s, l_s, ob, op,
    hog, h_ss, h_rs, ores, opair, opin, op_ss, op_rs, osend, orecv, o_ss, o_rs,
):
    i = lax.axis_index("seq")
    j = lax.axis_index("head")
    x = j // 2
    c = j % 2
    z = i // 4
    y = i % 4
    sib = 2 * x + (1 - c)

    def load(src, dst, sem):
        cp = pltpu.make_async_copy(src, dst, sem)
        cp.start()
        return cp

    def remote(src, dst, ss, rr, dev):
        return pltpu.make_async_remote_copy(
            src_ref=src, dst_ref=dst, send_sem=ss, recv_sem=rr,
            device_id=dev, device_id_type=MESH,
        )

    barrier = pltpu.get_barrier_semaphore()
    for dj in range(1, 8):
        pl.semaphore_signal(barrier, inc=1, device_id=(i, (j + dj) % 8), device_id_type=MESH)
    for di in range(1, 16):
        pl.semaphore_signal(barrier, inc=1, device_id=((i + di) % 16, j), device_id_type=MESH)

    c_wd = load(wd_h, wd, lsem.at[0])
    c_hid = load(hid_h, hid, lsem.at[1])

    sub128 = iota((128, 128), 0)
    lane128 = iota((128, 128), 1)
    sub16 = iota((16, 128), 0)
    hot = jnp.concatenate(
        [jnp.where(sub16 == own_r[b : b + 1, :], 1.0, 0.0) for b in range(8)], axis=0
    )
    hot_b = hot.astype(BF16)
    ahead = nn(hot_b, one_hot(sub128 < lane128))
    count = nn(hot_b, jnp.ones((128, 128), BF16)).astype(BF16)
    before = ((lane128 & 15) < (sub128 & 15)) | (
        ((lane128 & 15) == (sub128 & 15)) & ((lane128 >> 4) < (sub128 >> 4))
    )
    ahead = ahead + nn(one_hot(before), count)
    ends = nn(one_hot((iota((16, 128), 1) & 15) <= sub16), count)
    place = jnp.sum((hot * ahead).reshape(8, 16, 128), axis=1).astype(I32)
    dev = place & 7
    at = place >> 3
    rs[0:8, :] = dev * 128 + at
    key = dev * 16 + (at & 15)
    mine_at = rs[0:8, :] - j * 128
    off = off_r[...]
    digits, keys, marks, picks = [], [], [], []
    sub32 = iota((32, 128), 0)
    for b in range(8):
        one = slice(b, b + 1)
        high, low = (off[one] >> 7).astype(F32), (off[one] & 127).astype(F32)
        hb = hot[b * 16 : b * 16 + 16]
        digits.append(jnp.concatenate([hb * high, hb * low, hb], axis=0).astype(BF16))
        keys.append(one_hot(sub128 == key[one]))
        mark = jnp.where(sub32 == (off[one] >> 10), 1.0, 0.0)
        mark = jnp.where(sub32 == 17, ((off[one] >> 7) & 7).astype(F32), mark)
        mark = jnp.where(sub32 == 18, low, mark)
        marks.append(
            jnp.concatenate([jnp.zeros((64, 128), F32), mark, jnp.zeros((32, 128), F32)], axis=0)
            .astype(BF16)
        )
        picks.append(one_hot(sub128 == mine_at[one]))
    table = nt(jnp.concatenate(digits, axis=1), jnp.concatenate(keys, axis=1))
    feat[...] = nt(jnp.concatenate(picks, axis=1), jnp.concatenate(marks, axis=1))
    cells = jnp.where(table[32:48] > 0.5, table[0:16] * 128.0 + table[16:32], -1.0)
    for o in range(16):
        tsend[o] = jnp.broadcast_to(cells[o : o + 1, :], (8, 128))
    row_place = (iota((16, 128), 1) * 8 + j).astype(F32)
    owner_at = jnp.sum(
        jnp.where(row_place >= ends, 1.0, 0.0), axis=0, keepdims=True
    ).astype(I32)
    slot_at = owner_at * 16 + (iota((1, 128), 1) & 15)
    rs[8:9, :] = slot_at
    request = iota((32, 128), 0) & 15
    position = iota((32, 128), 0) >> 4
    for r in range(16):
        position = position + jnp.where(request == r, lens[r], 0)
    lane32 = iota((32, 128), 1)
    angle = position.astype(F32) * turn_rate(lane32)
    ntab[0] = jnp.cos(angle)
    ntab[1] = jnp.where((lane32 & 63) < 32, -1.0, 1.0) * jnp.sin(angle)

    c_wd.wait()
    c_uq = load(uq_h, uq, lsem.at[2])
    c_uk = load(uk_h, uk, lsem.at[3])
    npp[0] = nt(newh[...], wd[0:1152, :]).astype(BF16)
    npp[1, :, 0:896] = nt(newh[...], wd[1152:2048, :]).astype(BF16)
    tail = nt(newh[...], wd[2048:2112, :])
    npp[1, :, 896:1024] = jnp.concatenate([tail, tail], axis=1).astype(BF16)
    npp[1, :, 1024:1152] = jnp.zeros((32, 128), BF16)
    c_hid.wait()

    def k_copy(r):
        return pltpu.make_async_copy(cache_h.at[r], kc.at[r], ksem.at[r])

    @pl.loop(0, 16)
    def _(r):
        k_copy(r).start()

    c_uv = load(uv_h, uv, lsem.at[4])
    c_wo = load(wo_h, wo, lsem.at[5])
    @pl.loop(0, 2)
    def _(t):
        rows = pl.ds(pl.multiple_of(t * 512, 512), 512)
        h = hid[rows, :]
        part[rows, 0:512] = nt(h, wd[1536:2048, :]).astype(BF16)
        u = nt(h, wd[2048:2112, :])
        part[rows, 512:640] = jnp.concatenate([u, u], axis=1).astype(BF16)

    def npx_copy(dx):
        return remote(
            npx, npxr.at[dx], np_ss.at[dx], np_rs.at[dx], (i, 2 * ((x + dx) % 4) + c)
        )

    def permuted(first, second):
        ids = rs[0:8, :]
        top = [one_hot(sub128 == ids[b : b + 1, :] - first * 128) for b in range(8)]
        low = [one_hot(sub128 == ids[b : b + 1, :] - second * 128) for b in range(8)]
        pick = jnp.concatenate(
            [jnp.concatenate(top, axis=1), jnp.concatenate(low, axis=1)], axis=0
        )
        return nn(pick, part[...])

    def p_copy(dx):
        return remote(ps.at[dx], pr.at[dx], p_ss.at[dx], p_rs.at[dx], (i, sib))

    def via_copy(k):
        return remote(
            xs.at[2, pl.ds(64 * k, 64), :], xr.at[2, pl.ds(64 * k, 64), :],
            x_ss.at[k], x_rs.at[k], (i, 2 * ((x + 1 + 2 * k) % 4) + c),
        )

    def x_copy(dx, k):
        rows = pl.ds(64 * k, 64)
        return remote(
            xs.at[dx, rows, :], xr.at[dx, rows, :], x_ss.at[2 * dx + k], x_rs.at[2 * dx + k],
            (i, 2 * ((x + dx) % 4) + c),
        )

    @pl.loop(0, 2)
    def _(t):
        first, second = 2 + t, 1 - t
        both = permuted(2 * ((x + first) % 4) + 1 - c, 2 * ((x + second) % 4) + 1 - c)
        ps[first] = both[0:128].astype(BF16)
        ps[second] = both[128:256].astype(BF16)

    pl.semaphore_wait(barrier, 22)
    np_pair = remote(npp.at[1 - c], npair, np_ss.at[0], np_rs.at[0], (i, sib))
    np_pair.start()
    for dx in (2, 1, 3, 0):
        p_copy(dx).start()

    def t_copy(di):
        to = (i + di) % 16
        return remote(tsend.at[to], trecv.at[i], ts_sem.at[di], tr_sem.at[di], (to, j))

    both = permuted(2 * ((x + 2) % 4) + c, 2 * ((x + 1) % 4) + c)
    np_pair.wait_recv()
    npx[...] = (npp[c].astype(F32) + npair[...].astype(F32)).astype(BF16)
    for dx in (2, 1, 3):
        npx_copy(dx).start()
    p_copy(2).wait_recv()
    xs[2] = (both[0:128] + pr[2].astype(F32)).astype(BF16)
    via_copy(0).start()
    via_copy(1).start()
    for di in range(1, 16):
        t_copy(di).start()
    p_copy(1).wait_recv()
    up = both[128:256] + pr[1].astype(F32)
    xs[1, 64:128, :] = up[64:128].astype(BF16)
    x_copy(1, 1).start()
    both = permuted(2 * ((x + 3) % 4) + c, 2 * x + c)
    p_copy(3).wait_recv()
    down = both[0:128] + pr[3].astype(F32)
    xs[3, 0:64, :] = down[0:64].astype(BF16)
    x_copy(3, 0).start()
    p_copy(0).wait_recv()
    mine[...] = both[128:256] + pr[0].astype(F32)

    total = npx[...].astype(F32)
    for dx in (1, 3, 2):
        npx_copy(dx).wait_recv()
        total = total + npxr[dx].astype(F32)
    npfin[c] = total.astype(BF16)
    np_swap = remote(npfin.at[c], npfin.at[c], np_ss.at[4], np_rs.at[4], (i, sib))
    np_swap.start()
    via_copy(0).wait_recv()
    xs[1, 0:64, :] = (up[0:64] + xr[2, 0:64, :].astype(F32)).astype(BF16)
    x_copy(1, 0).start()
    via_copy(1).wait_recv()
    xs[3, 64:128, :] = (down[64:128] + xr[2, 64:128, :].astype(F32)).astype(BF16)
    x_copy(3, 1).start()
    np_swap_in = remote(npfin.at[1 - c], npfin.at[1 - c], np_ss.at[4], np_rs.at[4], (i, sib))
    np_swap_in.wait_recv()

    unit = LOG2E / (NOPE + ROPE) ** 0.5
    low32 = iota((32, 128), 1) < 64
    q_in = jnp.concatenate([npfin[0], npfin[1, :, 0:384]], axis=1).astype(F32)
    q_in = q_in * lax.rsqrt(jnp.mean(q_in * q_in, axis=1, keepdims=True) + 1e-6) * gain_q[...].astype(F32).reshape(1, QRANK)
    qls[...] = q_in.astype(BF16)
    k_in = npfin[1, :, 384:896].astype(F32)
    k_in = k_in * lax.rsqrt(jnp.mean(k_in * k_in, axis=1, keepdims=True) + 1e-6) * gain_kv[...].astype(F32).reshape(1, LATENT)
    newk[0:32, 0:512] = k_in.astype(BF16)
    newk[32:128, 0:512] = jnp.zeros((96, 512), BF16)
    u = npfin[1, :, 896:1024].astype(F32)
    u = u * ntab[0] + turned(u) * ntab[1]
    row32 = iota((32, 128), 0)
    own_lane = lane32 == 64 + (row32 & 15)
    late = (lane32 == 83) & (row32 >= 16)
    u = jnp.where(low32, u, jnp.where(own_lane | late, 1.0, 0.0))
    newk[0:32, 512:640] = u.astype(BF16)
    newk[32:128, 512:640] = one_hot(iota((96, 128), 1) == 80)
    other = (lane32 >= 64) & (lane32 < 81) & jnp.logical_not(own_lane)
    qex = jnp.where(other | ((lane32 == 83) & (row32 < 16)), HIDE, 0.0)

    c_uq.wait()
    c_uk.wait()

    def two_heads(p):
        q = nn(qls[...], uq[:, pl.ds(pl.multiple_of(p * 384, 384), 384)])
        t0, t1, t2 = q[:, 0:128], q[:, 128:256], q[:, 256:384]
        odd = jnp.where(low32, pltpu.roll(t1, 64, 1), pltpu.roll(t2, 64, 1))
        rope = jnp.where(low32, t1, t2)
        rope = rope * ntab[0] + turned(rope) * ntab[1]
        for s, (nope, rot) in enumerate(((t0, rope), (odd, pltpu.roll(rope, 64, 1)))):
            rows = pl.ds(pl.multiple_of(p * 64 + s * 32, 32), 32)
            ql[rows, 0:512] = (nn(nope.astype(BF16), uk[2 * p + s]) * unit).astype(BF16)
            ql[rows, 512:640] = jnp.where(low32, rot * unit, qex).astype(BF16)

    @pl.loop(0, 4)
    def _(p):
        for q in range(2):
            two_heads(2 * p + q)

    @pl.loop(0, 2)
    def _(t):
        n = iota((256, 512), 0) + t * 256
        want = ((n & 31) >> 1) * 32 + (n & 1) * 16 + (n >> 5)
        rows = pl.ds(pl.multiple_of(t * 256, 256), 256)
        qs[rows, :] = nn(one_hot(iota((256, 512), 1) == want), ql[...]).astype(BF16)

    at_src = tsend[i]
    trecv[i] = at_src
    for di in range(1, 16):
        src = (i + 16 - di) % 16
        remote(tsend.at[src], trecv.at[src], ts_sem.at[di], tr_sem.at[di], (src, j)).wait_recv()

    tall, wide = [], []
    for s in range(16):
        cell = trecv[s, 0:1, :].astype(I32)
        tall.append(one_hot(sub128 == (cell >> 7)))
        wide.append(one_hot(sub128 == (cell & 127)))
    taken = nt(jnp.concatenate(tall, axis=1), jnp.concatenate(wide, axis=1))
    length = jnp.zeros((128, 128), I32)
    weigh = jnp.where(iota((8, 128), 1) == 81, -128.0, 0.0)
    weigh = jnp.where(iota((8, 128), 1) == 82, -1.0, weigh)
    for r in range(16):
        length = length + jnp.where((sub128 >> 3) == r, lens[r], 0)
        weigh = weigh + jnp.where(iota((8, 128), 1) == 64 + r, lens[r], 0).astype(F32)
    seen = (sub128 & 7) * 128 + lane128 < length
    biasm[...] = jnp.where((taken < 0.5) & seen, 0.0, HIDE)

    snew[...] = nt(qs[...], newk[...])
    quarter = [one_hot((lane128 >> 5) == r) for r in range(4)]

    def cache_four(t):
        if True:
            for r in range(4):
                k_copy(4 * t + r).wait()
            rows = pl.ds(pl.multiple_of(t * 128, 128), 128)
            bias = biasm[pl.ds(pl.multiple_of(t * 32, 32), 32), :]
            s = [
                nn(qs[pl.ds(pl.multiple_of(t * 128 + r * 32, 32), 32), 0:576], kc[4 * t + r])
                for r in range(4)
            ]
            s = [
                jnp.concatenate(
                    [
                        s[r][:, g * 128 : (g + 1) * 128] + bias[8 * r + g : 8 * r + g + 1, :]
                        for r in range(4)
                    ],
                    axis=0,
                )
                for g in range(8)
            ]
            s.append(snew[rows, :])
            top = jnp.max(functools.reduce(jnp.maximum, s), axis=1, keepdims=True)
            m = jnp.broadcast_to(top, (128, 128))
            e = [jnp.exp2(v - m) for v in s]
            m_s[rows, :] = m
            l_s[rows, :] = functools.reduce(jnp.add, e)
            enew[rows, :] = e[8].astype(BF16)
            e = [v.T.astype(BF16) for v in e[0:8]]
            val = functools.reduce(
                jnp.add,
                [
                    nn(kc[4 * t + r, 0:512, :], jnp.concatenate([v * quarter[r] for v in e], axis=0))
                    for r in range(4)
                ],
            )
            acc[rows, :] = val.T

    total = mine[...]
    for dx in (1, 3):
        x_copy(dx, 0).wait_recv()
        x_copy(dx, 1).wait_recv()
        total = total + xr[dx].astype(F32)
    lat = total[:, 0:512]
    lat = lat * lax.rsqrt(jnp.mean(lat * lat, axis=1, keepdims=True) + 1e-6) * gain_kv[...].astype(F32).reshape(1, LATENT)
    tail = total[:, 512:640]
    marks = feat[...]
    at = jnp.where(lane128 == 81, 128.0, jnp.where(lane128 == 82, 1.0, 0.0))
    at = jnp.sum(marks * at, axis=1, keepdims=True)
    angle = at * turn_rate(lane128)
    sign = jnp.where((lane128 & 63) < 32, -1.0, 1.0)
    tail = tail * jnp.cos(angle) + turned(tail) * (sign * jnp.sin(angle))
    tail = jnp.where(lane128 < 64, tail, marks)
    rows_b = jnp.concatenate([lat, tail], axis=1).astype(BF16)
    spread = one_hot(iota((256, 128), 0) == rs[8:9, :])
    disp[...] = nn(spread, rows_b).astype(BF16)

    def d_copy(di):
        to = (i + di) % 16
        return remote(
            disp.at[pl.ds(pl.multiple_of(to * 16, 16), 16), :],
            slots.at[j, pl.ds(pl.multiple_of(i * 16, 16), 16), :],
            d_ss.at[di], d_rs.at[di], (to, j),
        )

    for di in range(1, 16):
        d_copy(di).start()
    at_me = pl.ds(pl.multiple_of(i * 16, 16), 16)
    slots[j, at_me, :] = disp[at_me, :]


    def g_half(block, k):
        return slots.at[block, pl.ds(128 * k, 128), :]

    def g_copy(block, k, ss, to):
        return remote(
            g_half(block, k), g_half(block, k), g_ss.at[ss], g_rs.at[block, k], (i, to)
        )

    def g_wait(block, k):
        g_copy(block, k, 0, sib).wait_recv()

    above, below, across = (2 * ((x + d) % 4) + c for d in (1, 3, 2))
    g_sent = []

    def g_send(block, k, to):
        g_sent.append((block, k, len(g_sent), to))
        g_copy(*g_sent[-1]).start()

    @pl.loop(0, 4)
    def _(t):
        cache_four(t)

        @pl.when(t == 0)
        def _():
            for di in range(1, 16):
                src = (i + 16 - di) % 16
                remote(
                    disp.at[pl.ds(pl.multiple_of(src * 16, 16), 16), :],
                    slots.at[j, pl.ds(pl.multiple_of(src * 16, 16), 16), :],
                    d_ss.at[di], d_rs.at[di], (src, j),
                ).wait_recv()
            marks = slots[j, :, 512:640].astype(F32)
            left = jnp.sum(marks * weigh[0:1, :], axis=1, keepdims=True)
            marks = jnp.where(
                iota((256, 128), 1) == 80, jnp.where(left > 0.5, 0.0, 1.0), marks
            )
            slots[j, :, 512:640] = marks.astype(BF16)
            g_send(j, 0, above)
            g_send(j, 1, below)
            g_send(j, 0, sib)
            g_send(j, 1, sib)

        @pl.when(t == 1)
        def _():
            g_copy(*g_sent[0]).wait_send()
            g_copy(*g_sent[1]).wait_send()
            g_send(j, 1, above)
            g_send(j, 0, below)

        @pl.when(t == 2)
        def _():
            g_wait(below, 0)
            g_send(below, 0, above)
            g_wait(above, 1)
            g_send(above, 1, below)
            g_send(below, 0, sib)
            g_send(above, 1, sib)

    acc[...] = acc[...] + nn(enew[...], newk[:, 0:512])

    def slot_part(first, second):
        q = qs[...]
        blocks = (first, second)
        s = [nt(q, slots[b]) for b in blocks]
        s = [v[:, g * 128 : (g + 1) * 128] for v in s for g in range(2)]
        old = m_s[...]
        top = jnp.max(functools.reduce(jnp.maximum, s), axis=1, keepdims=True)
        m = jnp.maximum(old, jnp.broadcast_to(top, (512, 128)))
        keep = jnp.exp2(old - m)
        e = [jnp.exp2(v - m) for v in s]
        m_s[...] = m
        l_s[...] = l_s[...] * keep + functools.reduce(jnp.add, e)
        e = [v.astype(BF16) for v in e]
        val = nn(jnp.concatenate(e[0:2], axis=1), slots[first, :, 0:512])
        val = val + nn(jnp.concatenate(e[2:4], axis=1), slots[second, :, 0:512])
        acc[...] = acc[...] * jnp.concatenate([keep] * 4, axis=1) + val

    @pl.loop(0, 4)
    def _(t):
        @pl.when(t == 1)
        def _():
            g_wait(below, 1)
            g_send(below, 1, sib)
            g_wait(above, 0)
            g_send(above, 0, sib)

        @pl.when(t == 3)
        def _():
            for k in range(2):
                g_wait(across, k)
                g_send(across, k, sib)

        chip = 2 * ((x + jnp.where(t == 1, 3, jnp.where(t == 2, 1, jnp.where(t == 3, 2, 0)))) % 4)
        for k in range(2):
            g_wait(chip + 1 - c, k)
        slot_part(chip + c, chip + 1 - c)

    @pl.loop(0, 2)
    def _(t):
        rows = pl.ds(pl.multiple_of(t * 256, 256), 256)
        ob[rows, :] = (
            acc[rows, :] * (1.0 / jnp.sum(l_s[rows, :], axis=1, keepdims=True))
        ).astype(BF16)

    @pl.loop(0, 2)
    def _(t):
        n = iota((256, 512), 0) + t * 256
        want = (n & 15) * 32 + (n >> 5) * 2 + ((n >> 4) & 1)
        rows = pl.ds(pl.multiple_of(t * 256, 256), 256)
        op[rows, :] = nn(one_hot(iota((256, 512), 1) == want), ob[...]).astype(BF16)

    c_uv.wait()
    c_wo.wait()

    def o_dev(dz, dy):
        return ((z + dz) % 4) * 4 + (y + dy) % 4

    def near(half, d):
        return o_dev(0, d) if half == 0 else o_dev(d, 0)

    def far(half, d):
        return o_dev(d, 0) if half == 0 else o_dev(0, d)

    def cross(half, n, f):
        return o_dev(f, n) if half == 0 else o_dev(n, f)

    h_sent = []

    def h_copy(half, piece, k, ss, to):
        ref = hog.at[half, piece, pl.ds(16 * k, 16), :]
        return remote(ref, ref, h_ss.at[ss], h_rs.at[half, piece, k], (to, j))

    def h_send(half, piece, k, to):
        cp = h_copy(half, piece, k, len(h_sent), to)
        cp.start()
        h_sent.append(cp)

    def h_wait(half, piece, k):
        h_copy(half, piece, k, 0, i).wait_recv()

    def far_first(half, piece):
        h_send(half, piece, 0, far(half, 1))
        h_send(half, piece, 1, far(half, 3))

    def far_rest(half, piece):
        h_send(half, piece, 1, far(half, 1))
        h_send(half, piece, 0, far(half, 3))

    def far_on(half, n):
        h_wait(half, cross(half, n, 3), 0)
        h_send(half, cross(half, n, 3), 0, far(half, 1))
        h_wait(half, cross(half, n, 1), 1)
        h_send(half, cross(half, n, 1), 1, far(half, 3))

    def far_end(half, n, f):
        if f != 1:
            h_wait(half, cross(half, n, f), 1)
        if f != 3:
            h_wait(half, cross(half, n, f), 0)

    halves = range(2)
    for half in halves:
        for h in range(8):
            hog[half, i, :, h * 128 : (h + 1) * 128] = nn(
                op[(half * 8 + h) * 32 : (half * 8 + h + 1) * 32, :], uv[half * 8 + h]
            ).astype(BF16)
        h_send(half, i, 0, near(half, 1))
        h_send(half, i, 1, near(half, 3))
        h_send(half, i, 1, near(half, 1))
        h_send(half, i, 0, near(half, 3))
    for half in halves:
        far_first(half, i)
    for half in halves:
        h_wait(half, near(half, 3), 0)
        h_send(half, near(half, 3), 0, near(half, 1))
        h_wait(half, near(half, 1), 1)
        h_send(half, near(half, 1), 1, near(half, 3))
    for half in halves:
        h_wait(half, near(half, 3), 1)
        far_first(half, near(half, 3))
        h_wait(half, near(half, 1), 0)
        far_first(half, near(half, 1))
    for half in halves:
        far_on(half, 0)
    for half in halves:
        far_rest(half, i)
    for half in halves:
        h_wait(half, near(half, 2), 0)
        h_wait(half, near(half, 2), 1)
        far_first(half, near(half, 2))
    for n in (3, 1):
        for half in halves:
            far_on(half, n)
    for n in (3, 1):
        for half in halves:
            far_rest(half, near(half, n))
    for half in halves:
        far_on(half, 2)
    for half in halves:
        far_rest(half, near(half, 2))

    def o_pair(t):
        return remote(opair.at[t], opin.at[t], op_ss.at[t], op_rs.at[t], (i, sib))

    def o_copy(t, to):
        return remote(osend.at[t], orecv.at[x], o_ss.at[t], o_rs.at[x], (i, 2 * to + c))

    def columns(t, row):
        four = pl.ds(row * 4, 4)
        res = nt(hog[0, four].reshape(128, 1024), wo[:, 0:1024])
        res = res + nt(hog[1, four].reshape(128, 1024), wo[:, 1024:2048])
        ores[t, :, 0:448] = res
        opair[t, :, 0:448] = ores[t, pl.ds(pl.multiple_of((1 - c) * 64, 64), 64), 0:448].astype(
            BF16
        )
        o_pair(t).start()

    def onward(t, row):
        o_pair(t).wait_recv()
        own_half = ores[t, pl.ds(pl.multiple_of(c * 64, 64), 64), :]
        osend[t] = (own_half + opin[t].astype(F32)).astype(BF16)

        @pl.when(row != x)
        def _():
            o_copy(t, row).start()

        @pl.when(row == x)
        def _():
            orecv[x] = osend[t]

    order = (0, 3, 1, 2)
    rows_at = [(z + dz) % 4 for dz in order]
    @pl.loop(0, 4)
    def _(t):
        for at, d in enumerate(order):

            @pl.when(t == at)
            def _():
                if d != 0:
                    for n in range(4):
                        far_end(0, n, d)
                for f in (1, 3, 2):
                    far_end(1, d, f)

        step = jnp.where(t == 1, 3, jnp.where(t == 2, 1, jnp.where(t == 3, 2, 0)))
        last = jnp.where(t == 2, 3, jnp.where(t == 3, 1, 0))
        columns(t, (z + step) % 4)

        @pl.when(t > 0)
        def _():
            onward(t - 1, (z + last) % 4)

    onward(3, rows_at[3])

    total = jnp.zeros((64, 448), F32)
    for dx in range(1, 4):
        src = (x + dx) % 4
        remote(osend.at[0], orecv.at[src], o_ss.at[0], o_rs.at[src], (i, 2 * src + c)).wait_recv()
    for src in range(4):
        total = total + orecv[src, :, 0:448].astype(F32)
    total = total.astype(BF16)
    for o in range(2):
        for s in range(2):
            out[s, o * 16 : (o + 1) * 16, :] = total[o * 32 + s * 16 : o * 32 + s * 16 + 16, :]

    for di in range(1, 16):
        t_copy(di).wait_send()
        d_copy(di).wait_send()
    np_pair.wait_send()
    np_swap.wait_send()
    for dx in range(4):
        p_copy(dx).wait_send()
    for dx in range(1, 4):
        npx_copy(dx).wait_send()
    for k in range(2):
        x_copy(1, k).wait_send()
        x_copy(3, k).wait_send()
        via_copy(k).wait_send()
    for one in g_sent[2:]:
        g_copy(*one).wait_send()
    for cp in h_sent:
        cp.wait_send()
    for t in range(4):
        o_pair(t).wait_send()

        @pl.when(rows_at[t] != x)
        def _():
            o_copy(t, rows_at[t]).wait_send()


def local(
    prompt_hidden, owner, offsets, cache, lengths, new_hidden, w_down,
    gain_q, gain_kv, w_uq, w_uk, w_uv, w_out,
):
    vm = pl.BlockSpec(memory_space=pltpu.VMEM)
    hb = pl.BlockSpec(memory_space=pl.ANY)
    V = pltpu.VMEM
    S = pltpu.SemaphoreType.DMA
    scratch = [
        V((1024, 896), BF16), V((2112, 896), BF16), V((1536, 3072), BF16), V((16, 128, 512), BF16),
        V((16, 576, 1024), BF16), V((16, 512, 128), BF16), V((448, 2048), BF16), S((6,)), S((16,)),
        V((16, 128), I32), V((128, 128), F32), V((16, 8, 128), F32), V((16, 8, 128), F32), S((16,)), S((16,)),
        V((2, 32, 1152), BF16), V((32, 1152), BF16), V((32, 1152), BF16), V((4, 32, 1152), BF16),
        V((2, 32, 1152), BF16), S((5,)), S((5,)), V((2, 32, 128), F32),
        V((1024, 640), BF16), V((4, 128, 640), BF16), V((4, 128, 640), BF16),
        V((4, 128, 640), BF16), V((4, 128, 640), BF16), V((128, 640), F32),
        S((4,)), S((4,)), S((8,)), S((8,)),
        V((256, 640), BF16), V((8, 256, 640), BF16), S((16,)), S((16,)), S((14,)), S((8, 2)),
        V((32, 1536), BF16), V((512, 640), BF16), V((512, 640), BF16), V((128, 640), BF16),
        V((512, 128), F32), V((512, 128), BF16), V((128, 128), F32), V((512, 512), F32), V((512, 128), F32), V((512, 128), F32),
        V((512, 512), BF16), V((512, 512), BF16),
        V((2, 16, 32, 1024), BF16), S((60,)), S((2, 16, 2)),
        V((4, 128, 512), F32), V((4, 64, 512), BF16), V((4, 64, 512), BF16), S((4,)), S((4,)),
        V((4, 64, 512), BF16), V((4, 64, 512), BF16), S((4,)), S((4,)),
    ]
    return pl.pallas_call(
        kernel,
        out_shape=jax.ShapeDtypeStruct((2, 32, 448), BF16),
        in_specs=[pl.BlockSpec(memory_space=pltpu.SMEM)] + [vm] * 5 + [hb] * 7,
        out_specs=vm,
        scratch_shapes=scratch,
        compiler_params=pltpu.CompilerParams(
            collective_id=0, has_side_effects=True, vmem_limit_bytes=60 * 1024 * 1024
        ),
    )(
        lengths, owner.reshape(8, 128), offsets.reshape(8, 128),
        gain_q, gain_kv,
        new_hidden.reshape(32, 896),
        prompt_hidden, w_down.T, w_uq, w_uk, jnp.swapaxes(cache, 1, 2), w_uv, w_out.T,
    )


def solution(mesh):
    in_specs = (
        P("seq", "head"), P("seq", None), P("seq"), P("seq", None, None), P("seq"),
        P(None, "seq", "head"), P("head", None), P(), P(), P(None, "head"),
        P("head", None, None), P("head", None, None), P("head", "seq"),
    )
    return jax.shard_map(
        local, mesh=mesh, in_specs=in_specs, out_specs=P(None, "head", "seq"), check_vma=False
    )
```

```python
import functools

import jax
import jax.numpy as jnp
from jax import lax
from jax.experimental import pallas as pl
from jax.experimental.pallas import tpu as pltpu
from jax.sharding import PartitionSpec as P

F32 = jnp.float32
BF16 = jnp.bfloat16
I32 = jnp.int32
MESH = pl.DeviceIdType.MESH
QRANK = 1536
LATENT = 512
ROPE = 64
NOPE = 128
VDIM = 128
HIDE = -1e30
LOG2E = 1.4426950408889634
LOG2_BASE = 13.287712379549449


def nt(a, b):
    return lax.dot_general(a, b, (((1,), (1,)), ((), ())), preferred_element_type=F32)


def nn(a, b):
    return jnp.dot(a, b, preferred_element_type=F32)


def iota(shape, dim):
    return lax.broadcasted_iota(I32, shape, dim)


def one_hot(cond):
    return jnp.where(cond, 1.0, 0.0).astype(BF16)


def turn_rate(lane):
    return jnp.exp2((lane & 31).astype(F32) * (-LOG2_BASE / (ROPE // 2)))


def turned(v):
    inner = (iota(v.shape, 1) & 63) < 32
    return jnp.where(inner, pltpu.roll(v, 96, 1), pltpu.roll(v, 32, 1))


def kernel(
    lens, own_h, off_h, gain_q_h, gain_kv_h, newh_h,
    hid_h, wd_h, uq_h, uk_h, cache_h, uv_h, wo_h,
    out,
    own_r, off_r, gain_q, gain_kv, newh, hid, wd, uq, uk, kc, uv, wo, lsem, ksem,
    rs, feat, tsend, trecv, ts_sem, tr_sem,
    npp, npair, npx, npxr, npfin, np_ss, np_rs, ntab,
    part, ps, pr, xs, xr, own, p_ss, p_rs, x_ss, x_rs,
    disp, slots, d_ss, d_rs, g_ss, g_rs,
    qls, ql, qs, newk, snew, enew, biasm, acc, m_s, l_s, ob, op,
    hog, h_ss, h_rs, ores, opair, opin, op_ss, op_rs, osend, orecv, o_ss, o_rs,
):
    i = lax.axis_index("seq")
    j = lax.axis_index("head")
    x = j // 2
    c = j % 2
    z = i // 4
    y = i % 4
    sib = 2 * x + (1 - c)

    def load(src, dst, sem):
        cp = pltpu.make_async_copy(src, dst, sem)
        cp.start()
        return cp

    def remote(src, dst, ss, rr, dev):
        return pltpu.make_async_remote_copy(
            src_ref=src, dst_ref=dst, send_sem=ss, recv_sem=rr,
            device_id=dev, device_id_type=MESH,
        )

    c_own = load(own_h, own_r, lsem.at[6])
    c_off = load(off_h, off_r, lsem.at[7])
    c_wd = load(wd_h, wd, lsem.at[0])
    c_new = load(newh_h, newh, lsem.at[8])
    c_hid = load(hid_h, hid, lsem.at[1])
    c_gq = load(gain_q_h, gain_q, lsem.at[9])
    c_gkv = load(gain_kv_h, gain_kv, lsem.at[10])

    barrier = pltpu.get_barrier_semaphore()
    for dj in range(1, 8):
        pl.semaphore_signal(barrier, inc=1, device_id=(i, (j + dj) % 8), device_id_type=MESH)
    for di in range(1, 16):
        pl.semaphore_signal(barrier, inc=1, device_id=((i + di) % 16, j), device_id_type=MESH)

    c_own.wait()
    c_off.wait()
    sub128 = iota((128, 128), 0)
    lane128 = iota((128, 128), 1)
    sub16 = iota((16, 128), 0)
    hot = jnp.concatenate(
        [jnp.where(sub16 == own_r[b : b + 1, :], 1.0, 0.0) for b in range(8)], axis=0
    )
    hot_b = hot.astype(BF16)
    ahead = nn(hot_b, one_hot(sub128 < lane128))
    count = nn(hot_b, jnp.ones((128, 128), BF16)).astype(BF16)
    before = ((lane128 & 15) < (sub128 & 15)) | (
        ((lane128 & 15) == (sub128 & 15)) & ((lane128 >> 4) < (sub128 >> 4))
    )
    ahead = ahead + nn(one_hot(before), count)
    ends = nn(one_hot((iota((16, 128), 1) & 15) <= sub16), count)
    place = jnp.sum((hot * ahead).reshape(8, 16, 128), axis=1).astype(I32)
    dev = place & 7
    at = place >> 3
    rs[0:8, :] = dev * 128 + at
    key = dev * 16 + (at & 15)
    mine_at = rs[0:8, :] - j * 128
    off = off_r[...]
    digits, keys, marks, picks = [], [], [], []
    sub32 = iota((32, 128), 0)
    for b in range(8):
        one = slice(b, b + 1)
        high, low = (off[one] >> 7).astype(F32), (off[one] & 127).astype(F32)
        hb = hot[b * 16 : b * 16 + 16]
        digits.append(jnp.concatenate([hb * high, hb * low, hb], axis=0).astype(BF16))
        keys.append(one_hot(sub128 == key[one]))
        mark = jnp.where(sub32 == (off[one] >> 10), 1.0, 0.0)
        mark = jnp.where(sub32 == 17, ((off[one] >> 7) & 7).astype(F32), mark)
        mark = jnp.where(sub32 == 18, low, mark)
        marks.append(
            jnp.concatenate([jnp.zeros((64, 128), F32), mark, jnp.zeros((32, 128), F32)], axis=0)
            .astype(BF16)
        )
        picks.append(one_hot(sub128 == mine_at[one]))
    table = nt(jnp.concatenate(digits, axis=1), jnp.concatenate(keys, axis=1))
    feat[...] = nt(jnp.concatenate(picks, axis=1), jnp.concatenate(marks, axis=1))
    cells = jnp.where(table[32:48] > 0.5, table[0:16] * 128.0 + table[16:32], -1.0)
    for o in range(16):
        tsend[o] = jnp.broadcast_to(cells[o : o + 1, :], (8, 128))
    row_place = (iota((16, 128), 1) * 8 + j).astype(F32)
    owner_at = jnp.sum(
        jnp.where(row_place >= ends, 1.0, 0.0), axis=0, keepdims=True
    ).astype(I32)
    slot_at = owner_at * 16 + (iota((1, 128), 1) & 15)
    rs[8:9, :] = slot_at
    request = iota((32, 128), 0) & 15
    position = iota((32, 128), 0) >> 4
    for r in range(16):
        position = position + jnp.where(request == r, lens[r], 0)
    lane32 = iota((32, 128), 1)
    angle = position.astype(F32) * turn_rate(lane32)
    ntab[0] = jnp.cos(angle)
    ntab[1] = jnp.where((lane32 & 63) < 32, -1.0, 1.0) * jnp.sin(angle)

    c_wd.wait()
    c_new.wait()
    c_uq = load(uq_h, uq, lsem.at[2])
    c_uk = load(uk_h, uk, lsem.at[3])
    npp[0] = nt(newh[...], wd[0:1152, :]).astype(BF16)
    npp[1, :, 0:896] = nt(newh[...], wd[1152:2048, :]).astype(BF16)
    tail = nt(newh[...], wd[2048:2112, :])
    npp[1, :, 896:1024] = jnp.concatenate([tail, tail], axis=1).astype(BF16)
    npp[1, :, 1024:1152] = jnp.zeros((32, 128), BF16)
    c_hid.wait()

    def k_copy(r):
        return pltpu.make_async_copy(cache_h.at[r], kc.at[r], ksem.at[r])

    @pl.loop(0, 16)
    def _(r):
        k_copy(r).start()

    c_uv = load(uv_h, uv, lsem.at[4])
    c_wo = load(wo_h, wo, lsem.at[5])
    @pl.loop(0, 2)
    def _(t):
        rows = pl.ds(pl.multiple_of(t * 512, 512), 512)
        h = hid[rows, :]
        part[rows, 0:512] = nt(h, wd[1536:2048, :]).astype(BF16)
        u = nt(h, wd[2048:2112, :])
        part[rows, 512:640] = jnp.concatenate([u, u], axis=1).astype(BF16)

    def npx_copy(dx):
        return remote(
            npx, npxr.at[dx], np_ss.at[dx], np_rs.at[dx], (i, 2 * ((x + dx) % 4) + c)
        )

    def permuted(first, second):
        ids = rs[0:8, :]
        top = [one_hot(sub128 == ids[b : b + 1, :] - first * 128) for b in range(8)]
        low = [one_hot(sub128 == ids[b : b + 1, :] - second * 128) for b in range(8)]
        pick = jnp.concatenate(
            [jnp.concatenate(top, axis=1), jnp.concatenate(low, axis=1)], axis=0
        )
        return nn(pick, part[...])

    def p_copy(dx):
        return remote(ps.at[dx], pr.at[dx], p_ss.at[dx], p_rs.at[dx], (i, sib))

    def via_copy(k):
        return remote(
            xs.at[2, pl.ds(64 * k, 64), :], xr.at[2, pl.ds(64 * k, 64), :],
            x_ss.at[k], x_rs.at[k], (i, 2 * ((x + 1 + 2 * k) % 4) + c),
        )

    def x_copy(dx, k):
        rows = pl.ds(64 * k, 64)
        return remote(
            xs.at[dx, rows, :], xr.at[dx, rows, :], x_ss.at[2 * dx + k], x_rs.at[2 * dx + k],
            (i, 2 * ((x + dx) % 4) + c),
        )

    @pl.loop(0, 2)
    def _(t):
        first, second = 2 + t, 1 - t
        both = permuted(2 * ((x + first) % 4) + 1 - c, 2 * ((x + second) % 4) + 1 - c)
        ps[first] = both[0:128].astype(BF16)
        ps[second] = both[128:256].astype(BF16)

    pl.semaphore_wait(barrier, 22)
    np_pair = remote(npp.at[1 - c], npair, np_ss.at[0], np_rs.at[0], (i, sib))
    np_pair.start()
    for dx in (2, 1, 3, 0):
        p_copy(dx).start()

    def t_copy(di):
        to = (i + di) % 16
        return remote(tsend.at[to], trecv.at[i], ts_sem.at[di], tr_sem.at[di], (to, j))

    @pl.loop(0, 2)
    def _(t):
        first, second = 2 + t, (1 - t) % 4
        both = permuted(2 * ((x + first) % 4) + c, 2 * ((x + second) % 4) + c)
        own[first] = both[0:128]
        own[second] = both[128:256]

        @pl.when(t == 0)
        def _():
            np_pair.wait_recv()
            npx[...] = (npp[c].astype(F32) + npair[...].astype(F32)).astype(BF16)
            for dx in (2, 1, 3):
                npx_copy(dx).start()
            p_copy(2).wait_recv()
            xs[2] = (own[2] + pr[2].astype(F32)).astype(BF16)
            via_copy(0).start()
            via_copy(1).start()
            for di in range(1, 16):
                t_copy(di).start()
            p_copy(1).wait_recv()
            own[1] = own[1] + pr[1].astype(F32)
            xs[1, 64:128, :] = own[1, 64:128, :].astype(BF16)
            x_copy(1, 1).start()

    p_copy(3).wait_recv()
    own[3] = own[3] + pr[3].astype(F32)
    xs[3, 0:64, :] = own[3, 0:64, :].astype(BF16)
    x_copy(3, 0).start()
    p_copy(0).wait_recv()
    own[0] = own[0] + pr[0].astype(F32)

    total = npx[...].astype(F32)
    for dx in (1, 3, 2):
        npx_copy(dx).wait_recv()
        total = total + npxr[dx].astype(F32)
    npfin[c] = total.astype(BF16)
    np_swap = remote(npfin.at[c], npfin.at[c], np_ss.at[4], np_rs.at[4], (i, sib))
    np_swap.start()
    via_copy(0).wait_recv()
    xs[1, 0:64, :] = (own[1, 0:64, :] + xr[2, 0:64, :].astype(F32)).astype(BF16)
    x_copy(1, 0).start()
    via_copy(1).wait_recv()
    xs[3, 64:128, :] = (own[3, 64:128, :] + xr[2, 64:128, :].astype(F32)).astype(BF16)
    x_copy(3, 1).start()
    np_swap_in = remote(npfin.at[1 - c], npfin.at[1 - c], np_ss.at[4], np_rs.at[4], (i, sib))
    np_swap_in.wait_recv()

    unit = LOG2E / (NOPE + ROPE) ** 0.5
    c_gq.wait()
    c_gkv.wait()
    low32 = iota((32, 128), 1) < 64
    q_in = jnp.concatenate([npfin[0], npfin[1, :, 0:384]], axis=1).astype(F32)
    q_in = q_in * lax.rsqrt(jnp.mean(q_in * q_in, axis=1, keepdims=True) + 1e-6) * gain_q[...].astype(F32).reshape(1, QRANK)
    qls[...] = q_in.astype(BF16)
    k_in = npfin[1, :, 384:896].astype(F32)
    k_in = k_in * lax.rsqrt(jnp.mean(k_in * k_in, axis=1, keepdims=True) + 1e-6) * gain_kv[...].astype(F32).reshape(1, LATENT)
    newk[0:32, 0:512] = k_in.astype(BF16)
    newk[32:128, 0:512] = jnp.zeros((96, 512), BF16)
    u = npfin[1, :, 896:1024].astype(F32)
    u = u * ntab[0] + turned(u) * ntab[1]
    row32 = iota((32, 128), 0)
    own_lane = lane32 == 64 + (row32 & 15)
    late = (lane32 == 83) & (row32 >= 16)
    u = jnp.where(low32, u, jnp.where(own_lane | late, 1.0, 0.0))
    newk[0:32, 512:640] = u.astype(BF16)
    newk[32:128, 512:640] = one_hot(iota((96, 128), 1) == 80)
    other = (lane32 >= 64) & (lane32 < 81) & jnp.logical_not(own_lane)
    qex = jnp.where(other | ((lane32 == 83) & (row32 < 16)), HIDE, 0.0)

    c_uq.wait()
    c_uk.wait()

    def two_heads(p):
        q = nn(qls[...], uq[:, pl.ds(pl.multiple_of(p * 384, 384), 384)])
        t0, t1, t2 = q[:, 0:128], q[:, 128:256], q[:, 256:384]
        odd = jnp.where(low32, pltpu.roll(t1, 64, 1), pltpu.roll(t2, 64, 1))
        rope = jnp.where(low32, t1, t2)
        rope = rope * ntab[0] + turned(rope) * ntab[1]
        for s, (nope, rot) in enumerate(((t0, rope), (odd, pltpu.roll(rope, 64, 1)))):
            rows = pl.ds(pl.multiple_of(p * 64 + s * 32, 32), 32)
            ql[rows, 0:512] = (nn(nope.astype(BF16), uk[2 * p + s]) * unit).astype(BF16)
            ql[rows, 512:640] = jnp.where(low32, rot * unit, qex).astype(BF16)

    @pl.loop(0, 4)
    def _(p):
        for q in range(2):
            two_heads(2 * p + q)

    @pl.loop(0, 2)
    def _(t):
        n = iota((256, 512), 0) + t * 256
        want = ((n & 31) >> 1) * 32 + (n & 1) * 16 + (n >> 5)
        rows = pl.ds(pl.multiple_of(t * 256, 256), 256)
        qs[rows, :] = nn(one_hot(iota((256, 512), 1) == want), ql[...]).astype(BF16)

    at_src = tsend[i]
    trecv[i] = at_src
    for di in range(1, 16):
        src = (i + 16 - di) % 16
        remote(tsend.at[src], trecv.at[src], ts_sem.at[di], tr_sem.at[di], (src, j)).wait_recv()

    tall, wide = [], []
    for s in range(16):
        cell = trecv[s, 0:1, :].astype(I32)
        tall.append(one_hot(sub128 == (cell >> 7)))
        wide.append(one_hot(sub128 == (cell & 127)))
    taken = nt(jnp.concatenate(tall, axis=1), jnp.concatenate(wide, axis=1))
    length = jnp.zeros((128, 128), I32)
    weigh = jnp.where(iota((8, 128), 1) == 81, -128.0, 0.0)
    weigh = jnp.where(iota((8, 128), 1) == 82, -1.0, weigh)
    for r in range(16):
        length = length + jnp.where((sub128 >> 3) == r, lens[r], 0)
        weigh = weigh + jnp.where(iota((8, 128), 1) == 64 + r, lens[r], 0).astype(F32)
    seen = (sub128 & 7) * 128 + lane128 < length
    biasm[...] = jnp.where((taken < 0.5) & seen, 0.0, HIDE)

    snew[...] = nt(qs[...], newk[...])
    quarter = [one_hot((lane128 >> 5) == r) for r in range(4)]

    def cache_four(t):
        if True:
            for r in range(4):
                k_copy(4 * t + r).wait()
            rows = pl.ds(pl.multiple_of(t * 128, 128), 128)
            bias = biasm[pl.ds(pl.multiple_of(t * 32, 32), 32), :]
            s = [
                nn(qs[pl.ds(pl.multiple_of(t * 128 + r * 32, 32), 32), 0:576], kc[4 * t + r])
                for r in range(4)
            ]
            s = [
                jnp.concatenate(
                    [
                        s[r][:, g * 128 : (g + 1) * 128] + bias[8 * r + g : 8 * r + g + 1, :]
                        for r in range(4)
                    ],
                    axis=0,
                )
                for g in range(8)
            ]
            s.append(snew[rows, :])
            top = jnp.max(functools.reduce(jnp.maximum, s), axis=1, keepdims=True)
            m = jnp.broadcast_to(top, (128, 128))
            e = [jnp.exp2(v - m) for v in s]
            m_s[rows, :] = m
            l_s[rows, :] = functools.reduce(jnp.add, e)
            enew[rows, :] = e[8].astype(BF16)
            e = [v.T.astype(BF16) for v in e[0:8]]
            val = functools.reduce(
                jnp.add,
                [
                    nn(kc[4 * t + r, 0:512, :], jnp.concatenate([v * quarter[r] for v in e], axis=0))
                    for r in range(4)
                ],
            )
            acc[rows, :] = val.T

    total = own[0]
    for dx in (1, 3):
        x_copy(dx, 0).wait_recv()
        x_copy(dx, 1).wait_recv()
        total = total + xr[dx].astype(F32)
    lat = total[:, 0:512]
    lat = lat * lax.rsqrt(jnp.mean(lat * lat, axis=1, keepdims=True) + 1e-6) * gain_kv[...].astype(F32).reshape(1, LATENT)
    tail = total[:, 512:640]
    marks = feat[...]
    at = jnp.where(lane128 == 81, 128.0, jnp.where(lane128 == 82, 1.0, 0.0))
    at = jnp.sum(marks * at, axis=1, keepdims=True)
    angle = at * turn_rate(lane128)
    sign = jnp.where((lane128 & 63) < 32, -1.0, 1.0)
    tail = tail * jnp.cos(angle) + turned(tail) * (sign * jnp.sin(angle))
    tail = jnp.where(lane128 < 64, tail, marks)
    rows_b = jnp.concatenate([lat, tail], axis=1).astype(BF16)
    spread = one_hot(iota((256, 128), 0) == rs[8:9, :])
    disp[...] = nn(spread, rows_b).astype(BF16)

    def d_copy(di):
        to = (i + di) % 16
        return remote(
            disp.at[pl.ds(pl.multiple_of(to * 16, 16), 16), :],
            slots.at[j, pl.ds(pl.multiple_of(i * 16, 16), 16), :],
            d_ss.at[di], d_rs.at[di], (to, j),
        )

    for di in range(1, 16):
        d_copy(di).start()
    at_me = pl.ds(pl.multiple_of(i * 16, 16), 16)
    slots[j, at_me, :] = disp[at_me, :]


    def g_half(block, k):
        return slots.at[block, pl.ds(128 * k, 128), :]

    def g_copy(block, k, ss, to):
        return remote(
            g_half(block, k), g_half(block, k), g_ss.at[ss], g_rs.at[block, k], (i, to)
        )

    def g_wait(block, k):
        g_copy(block, k, 0, sib).wait_recv()

    above, below, across = (2 * ((x + d) % 4) + c for d in (1, 3, 2))
    g_sent = []

    def g_send(block, k, to):
        g_sent.append((block, k, len(g_sent), to))
        g_copy(*g_sent[-1]).start()

    @pl.loop(0, 4)
    def _(t):
        cache_four(t)

        @pl.when(t == 0)
        def _():
            for di in range(1, 16):
                src = (i + 16 - di) % 16
                remote(
                    disp.at[pl.ds(pl.multiple_of(src * 16, 16), 16), :],
                    slots.at[j, pl.ds(pl.multiple_of(src * 16, 16), 16), :],
                    d_ss.at[di], d_rs.at[di], (src, j),
                ).wait_recv()
            marks = slots[j, :, 512:640].astype(F32)
            left = jnp.sum(marks * weigh[0:1, :], axis=1, keepdims=True)
            marks = jnp.where(
                iota((256, 128), 1) == 80, jnp.where(left > 0.5, 0.0, 1.0), marks
            )
            slots[j, :, 512:640] = marks.astype(BF16)
            g_send(j, 0, above)
            g_send(j, 1, below)
            g_send(j, 0, sib)
            g_send(j, 1, sib)

        @pl.when(t == 1)
        def _():
            g_copy(*g_sent[0]).wait_send()
            g_copy(*g_sent[1]).wait_send()
            g_send(j, 1, above)
            g_send(j, 0, below)

        @pl.when(t == 2)
        def _():
            g_wait(below, 0)
            g_send(below, 0, above)
            g_wait(above, 1)
            g_send(above, 1, below)
            g_send(below, 0, sib)
            g_send(above, 1, sib)

    acc[...] = acc[...] + nn(enew[...], newk[:, 0:512])

    def slot_part(first, second):
        q = qs[...]
        blocks = (first, second)
        s = [nt(q, slots[b]) for b in blocks]
        s = [v[:, g * 128 : (g + 1) * 128] for v in s for g in range(2)]
        old = m_s[...]
        top = jnp.max(functools.reduce(jnp.maximum, s), axis=1, keepdims=True)
        m = jnp.maximum(old, jnp.broadcast_to(top, (512, 128)))
        keep = jnp.exp2(old - m)
        e = [jnp.exp2(v - m) for v in s]
        m_s[...] = m
        l_s[...] = l_s[...] * keep + functools.reduce(jnp.add, e)
        e = [v.astype(BF16) for v in e]
        val = nn(jnp.concatenate(e[0:2], axis=1), slots[first, :, 0:512])
        val = val + nn(jnp.concatenate(e[2:4], axis=1), slots[second, :, 0:512])
        acc[...] = acc[...] * jnp.concatenate([keep] * 4, axis=1) + val

    @pl.loop(0, 4)
    def _(t):
        @pl.when(t == 1)
        def _():
            g_wait(below, 1)
            g_send(below, 1, sib)
            g_wait(above, 0)
            g_send(above, 0, sib)

        @pl.when(t == 3)
        def _():
            for k in range(2):
                g_wait(across, k)
                g_send(across, k, sib)

        chip = 2 * ((x + jnp.where(t == 1, 3, jnp.where(t == 2, 1, jnp.where(t == 3, 2, 0)))) % 4)
        for k in range(2):
            g_wait(chip + 1 - c, k)
        slot_part(chip + c, chip + 1 - c)

    @pl.loop(0, 2)
    def _(t):
        rows = pl.ds(pl.multiple_of(t * 256, 256), 256)
        ob[rows, :] = (
            acc[rows, :] * (1.0 / jnp.sum(l_s[rows, :], axis=1, keepdims=True))
        ).astype(BF16)

    @pl.loop(0, 2)
    def _(t):
        n = iota((256, 512), 0) + t * 256
        want = (n & 15) * 32 + (n >> 5) * 2 + ((n >> 4) & 1)
        rows = pl.ds(pl.multiple_of(t * 256, 256), 256)
        op[rows, :] = nn(one_hot(iota((256, 512), 1) == want), ob[...]).astype(BF16)

    c_uv.wait()
    c_wo.wait()

    def o_dev(dz, dy):
        return ((z + dz) % 4) * 4 + (y + dy) % 4

    def near(half, d):
        return o_dev(0, d) if half == 0 else o_dev(d, 0)

    def far(half, d):
        return o_dev(d, 0) if half == 0 else o_dev(0, d)

    def cross(half, n, f):
        return o_dev(f, n) if half == 0 else o_dev(n, f)

    h_sent = []

    def h_copy(half, piece, k, ss, to):
        ref = hog.at[half, piece, pl.ds(16 * k, 16), :]
        return remote(ref, ref, h_ss.at[ss], h_rs.at[half, piece, k], (to, j))

    def h_send(half, piece, k, to):
        cp = h_copy(half, piece, k, len(h_sent), to)
        cp.start()
        h_sent.append(cp)

    def h_wait(half, piece, k):
        h_copy(half, piece, k, 0, i).wait_recv()

    def far_first(half, piece):
        h_send(half, piece, 0, far(half, 1))
        h_send(half, piece, 1, far(half, 3))

    def far_rest(half, piece):
        h_send(half, piece, 1, far(half, 1))
        h_send(half, piece, 0, far(half, 3))

    def far_on(half, n):
        h_wait(half, cross(half, n, 3), 0)
        h_send(half, cross(half, n, 3), 0, far(half, 1))
        h_wait(half, cross(half, n, 1), 1)
        h_send(half, cross(half, n, 1), 1, far(half, 3))

    def far_end(half, n, f):
        if f != 1:
            h_wait(half, cross(half, n, f), 1)
        if f != 3:
            h_wait(half, cross(half, n, f), 0)

    halves = range(2)
    for half in halves:

        @pl.loop(0, 2)
        def _(t):
            for h in range(4):
                at = t * 4 + h
                rows = pl.ds(pl.multiple_of((half * 8 + at) * 32, 32), 32)
                hog[half, i, :, pl.ds(pl.multiple_of(at * 128, 128), 128)] = nn(
                    op[rows, :], uv[half * 8 + at]
                ).astype(BF16)

        h_send(half, i, 0, near(half, 1))
        h_send(half, i, 1, near(half, 3))
        h_send(half, i, 1, near(half, 1))
        h_send(half, i, 0, near(half, 3))
    for half in halves:
        far_first(half, i)
    for half in halves:
        h_wait(half, near(half, 3), 0)
        h_send(half, near(half, 3), 0, near(half, 1))
        h_wait(half, near(half, 1), 1)
        h_send(half, near(half, 1), 1, near(half, 3))
    for half in halves:
        h_wait(half, near(half, 3), 1)
        far_first(half, near(half, 3))
        h_wait(half, near(half, 1), 0)
        far_first(half, near(half, 1))
    for half in halves:
        far_on(half, 0)
    for half in halves:
        far_rest(half, i)
    for half in halves:
        h_wait(half, near(half, 2), 0)
        h_wait(half, near(half, 2), 1)
        far_first(half, near(half, 2))
    for n in (3, 1):
        for half in halves:
            far_on(half, n)
    for n in (3, 1):
        for half in halves:
            far_rest(half, near(half, n))
    for half in halves:
        far_on(half, 2)
    for half in halves:
        far_rest(half, near(half, 2))

    def o_pair(t):
        return remote(opair.at[t], opin.at[t], op_ss.at[t], op_rs.at[t], (i, sib))

    def o_copy(t, to):
        return remote(osend.at[t], orecv.at[x], o_ss.at[t], o_rs.at[x], (i, 2 * to + c))

    def columns(t, row):
        four = pl.ds(row * 4, 4)
        res = nt(hog[0, four].reshape(128, 1024), wo[:, 0:1024])
        res = res + nt(hog[1, four].reshape(128, 1024), wo[:, 1024:2048])
        ores[t, :, 0:448] = res
        opair[t, :, 0:448] = ores[t, pl.ds(pl.multiple_of((1 - c) * 64, 64), 64), 0:448].astype(
            BF16
        )
        o_pair(t).start()

    def onward(t, row):
        o_pair(t).wait_recv()
        own_half = ores[t, pl.ds(pl.multiple_of(c * 64, 64), 64), :]
        osend[t] = (own_half + opin[t].astype(F32)).astype(BF16)

        @pl.when(row != x)
        def _():
            o_copy(t, row).start()

        @pl.when(row == x)
        def _():
            orecv[x] = osend[t]

    order = (0, 3, 1, 2)
    rows_at = [(z + dz) % 4 for dz in order]
    @pl.loop(0, 4)
    def _(t):
        for at, d in enumerate(order):

            @pl.when(t == at)
            def _():
                if d != 0:
                    for n in range(4):
                        far_end(0, n, d)
                for f in (1, 3, 2):
                    far_end(1, d, f)

        step = jnp.where(t == 1, 3, jnp.where(t == 2, 1, jnp.where(t == 3, 2, 0)))
        last = jnp.where(t == 2, 3, jnp.where(t == 3, 1, 0))
        columns(t, (z + step) % 4)

        @pl.when(t > 0)
        def _():
            onward(t - 1, (z + last) % 4)

    onward(3, rows_at[3])

    total = jnp.zeros((64, 448), F32)
    for dx in range(1, 4):
        src = (x + dx) % 4
        remote(osend.at[0], orecv.at[src], o_ss.at[0], o_rs.at[src], (i, 2 * src + c)).wait_recv()
    for src in range(4):
        total = total + orecv[src, :, 0:448].astype(F32)
    total = total.astype(BF16)
    for o in range(2):
        for s in range(2):
            out[s, o * 16 : (o + 1) * 16, :] = total[o * 32 + s * 16 : o * 32 + s * 16 + 16, :]

    for di in range(1, 16):
        t_copy(di).wait_send()
        d_copy(di).wait_send()
    np_pair.wait_send()
    np_swap.wait_send()
    for dx in range(4):
        p_copy(dx).wait_send()
    for dx in range(1, 4):
        npx_copy(dx).wait_send()
    for k in range(2):
        x_copy(1, k).wait_send()
        x_copy(3, k).wait_send()
        via_copy(k).wait_send()
    for one in g_sent[2:]:
        g_copy(*one).wait_send()
    for cp in h_sent:
        cp.wait_send()
    for t in range(4):
        o_pair(t).wait_send()

        @pl.when(rows_at[t] != x)
        def _():
            o_copy(t, rows_at[t]).wait_send()


def local(
    prompt_hidden, owner, offsets, cache, lengths, new_hidden, w_down,
    gain_q, gain_kv, w_uq, w_uk, w_uv, w_out,
):
    vm = pl.BlockSpec(memory_space=pltpu.VMEM)
    hb = pl.BlockSpec(memory_space=pl.ANY)
    V = pltpu.VMEM
    S = pltpu.SemaphoreType.DMA
    scratch = [
        V((8, 128), I32), V((8, 128), I32), V((QRANK,), BF16), V((LATENT,), BF16), V((32, 896), BF16),
        V((1024, 896), BF16), V((2112, 896), BF16), V((1536, 3072), BF16), V((16, 128, 512), BF16),
        V((16, 576, 1024), BF16), V((16, 512, 128), BF16), V((448, 2048), BF16), S((11,)), S((16,)),
        V((16, 128), I32), V((128, 128), F32), V((16, 8, 128), F32), V((16, 8, 128), F32), S((16,)), S((16,)),
        V((2, 32, 1152), BF16), V((32, 1152), BF16), V((32, 1152), BF16), V((4, 32, 1152), BF16),
        V((2, 32, 1152), BF16), S((5,)), S((5,)), V((2, 32, 128), F32),
        V((1024, 640), BF16), V((4, 128, 640), BF16), V((4, 128, 640), BF16),
        V((4, 128, 640), BF16), V((4, 128, 640), BF16), V((4, 128, 640), F32),
        S((4,)), S((4,)), S((8,)), S((8,)),
        V((256, 640), BF16), V((8, 256, 640), BF16), S((16,)), S((16,)), S((14,)), S((8, 2)),
        V((32, 1536), BF16), V((512, 640), BF16), V((512, 640), BF16), V((128, 640), BF16),
        V((512, 128), F32), V((512, 128), BF16), V((128, 128), F32), V((512, 512), F32), V((512, 128), F32), V((512, 128), F32),
        V((512, 512), BF16), V((512, 512), BF16),
        V((2, 16, 32, 1024), BF16), S((60,)), S((2, 16, 2)),
        V((4, 128, 512), F32), V((4, 64, 512), BF16), V((4, 64, 512), BF16), S((4,)), S((4,)),
        V((4, 64, 512), BF16), V((4, 64, 512), BF16), S((4,)), S((4,)),
    ]
    return pl.pallas_call(
        kernel,
        out_shape=jax.ShapeDtypeStruct((2, 32, 448), BF16),
        in_specs=[pl.BlockSpec(memory_space=pltpu.SMEM)] + [hb] * 12,
        out_specs=vm,
        scratch_shapes=scratch,
        compiler_params=pltpu.CompilerParams(
            collective_id=0, has_side_effects=True, vmem_limit_bytes=60 * 1024 * 1024
        ),
    )(
        lengths, owner.reshape(8, 128), offsets.reshape(8, 128),
        gain_q, gain_kv,
        new_hidden.reshape(32, 896),
        prompt_hidden, w_down.T, w_uq, w_uk, jnp.swapaxes(cache, 1, 2), w_uv, w_out.T,
    )


def solution(mesh):
    in_specs = (
        P("seq", "head"), P("seq", None), P("seq"), P("seq", None, None), P("seq"),
        P(None, "seq", "head"), P("head", None), P(), P(), P(None, "head"),
        P("head", None, None), P("head", None, None), P("head", "seq"),
    )
    return jax.shard_map(
        local, mesh=mesh, in_specs=in_specs, out_specs=P(None, "head", "seq"), check_vma=False
    )
```

```python
import functools

import jax
import jax.numpy as jnp
from jax import lax
from jax.experimental import pallas as pl
from jax.experimental.pallas import tpu as pltpu
from jax.sharding import PartitionSpec as P

F32 = jnp.float32
BF16 = jnp.bfloat16
I32 = jnp.int32
MESH = pl.DeviceIdType.MESH
QRANK = 1536
LATENT = 512
ROPE = 64
NOPE = 128
VDIM = 128
HIDE = -1e30
LOG2E = 1.4426950408889634
LOG2_BASE = 13.287712379549449


def nt(a, b):
    return lax.dot_general(a, b, (((1,), (1,)), ((), ())), preferred_element_type=F32)


def nn(a, b):
    return jnp.dot(a, b, preferred_element_type=F32)


def iota(shape, dim):
    return lax.broadcasted_iota(I32, shape, dim)


def one_hot(cond):
    return jnp.where(cond, 1.0, 0.0).astype(BF16)


def turn_rate(lane):
    return jnp.exp2((lane & 31).astype(F32) * (-LOG2_BASE / (ROPE // 2)))


def turned(v):
    inner = (iota(v.shape, 1) & 63) < 32
    return jnp.where(inner, pltpu.roll(v, 96, 1), pltpu.roll(v, 32, 1))


def kernel(
    lens, own_h, off_h, gain_q_h, gain_kv_h, newh_h,
    hid_h, wd_h, uq_h, uk_h, cache_h, uv_h, wo_h,
    out,
    own_r, off_r, gain_q, gain_kv, newh, hid, wd, uq, uk, kc, uv, wo, lsem, ksem,
    rs, feat, tsend, trecv, ts_sem, tr_sem,
    npp, npair, npx, npxr, npfin, np_ss, np_rs, ntab,
    part, ps, pr, xs, xr, own, p_ss, p_rs, x_ss, x_rs,
    disp, slots, d_ss, d_rs, g_ss, g_rs,
    qls, ql, qs, newk, snew, enew, biasm, acc, m_s, l_s, ob, op,
    hog, h_ss, h_rs, ores, opair, opin, op_ss, op_rs, osend, orecv, o_ss, o_rs,
):
    i = lax.axis_index("seq")
    j = lax.axis_index("head")
    x = j // 2
    c = j % 2
    z = i // 4
    y = i % 4
    sib = 2 * x + (1 - c)

    def load(src, dst, sem):
        cp = pltpu.make_async_copy(src, dst, sem)
        cp.start()
        return cp

    def remote(src, dst, ss, rr, dev):
        return pltpu.make_async_remote_copy(
            src_ref=src, dst_ref=dst, send_sem=ss, recv_sem=rr,
            device_id=dev, device_id_type=MESH,
        )

    c_own = load(own_h, own_r, lsem.at[6])
    c_off = load(off_h, off_r, lsem.at[7])
    c_wd = load(wd_h, wd, lsem.at[0])
    c_new = load(newh_h, newh, lsem.at[8])
    c_hid = load(hid_h, hid, lsem.at[1])
    c_gq = load(gain_q_h, gain_q, lsem.at[9])
    c_gkv = load(gain_kv_h, gain_kv, lsem.at[10])

    barrier = pltpu.get_barrier_semaphore()
    for dj in range(1, 8):
        pl.semaphore_signal(barrier, inc=1, device_id=(i, (j + dj) % 8), device_id_type=MESH)
    for di in range(1, 16):
        pl.semaphore_signal(barrier, inc=1, device_id=((i + di) % 16, j), device_id_type=MESH)

    c_own.wait()
    c_off.wait()
    sub128 = iota((128, 128), 0)
    lane128 = iota((128, 128), 1)
    sub16 = iota((16, 128), 0)
    hot = jnp.concatenate(
        [jnp.where(sub16 == own_r[b : b + 1, :], 1.0, 0.0) for b in range(8)], axis=0
    )
    hot_b = hot.astype(BF16)
    ahead = nn(hot_b, one_hot(sub128 < lane128))
    count = nn(hot_b, jnp.ones((128, 128), BF16)).astype(BF16)
    before = ((lane128 & 15) < (sub128 & 15)) | (
        ((lane128 & 15) == (sub128 & 15)) & ((lane128 >> 4) < (sub128 >> 4))
    )
    ahead = ahead + nn(one_hot(before), count)
    ends = nn(one_hot((iota((16, 128), 1) & 15) <= sub16), count)
    place = jnp.sum((hot * ahead).reshape(8, 16, 128), axis=1).astype(I32)
    dev = place & 7
    at = place >> 3
    rs[0:8, :] = dev * 128 + at
    key = dev * 16 + (at & 15)
    mine_at = rs[0:8, :] - j * 128
    off = off_r[...]
    digits, keys, marks, picks = [], [], [], []
    sub32 = iota((32, 128), 0)
    for b in range(8):
        one = slice(b, b + 1)
        high, low = (off[one] >> 7).astype(F32), (off[one] & 127).astype(F32)
        hb = hot[b * 16 : b * 16 + 16]
        digits.append(jnp.concatenate([hb * high, hb * low, hb], axis=0).astype(BF16))
        keys.append(one_hot(sub128 == key[one]))
        mark = jnp.where(sub32 == (off[one] >> 10), 1.0, 0.0)
        mark = jnp.where(sub32 == 17, ((off[one] >> 7) & 7).astype(F32), mark)
        mark = jnp.where(sub32 == 18, low, mark)
        marks.append(
            jnp.concatenate([jnp.zeros((64, 128), F32), mark, jnp.zeros((32, 128), F32)], axis=0)
            .astype(BF16)
        )
        picks.append(one_hot(sub128 == mine_at[one]))
    table = nt(jnp.concatenate(digits, axis=1), jnp.concatenate(keys, axis=1))
    feat[...] = nt(jnp.concatenate(picks, axis=1), jnp.concatenate(marks, axis=1))
    cells = jnp.where(table[32:48] > 0.5, table[0:16] * 128.0 + table[16:32], -1.0)
    for o in range(16):
        tsend[o] = jnp.broadcast_to(cells[o : o + 1, :], (8, 128))
    row_place = (iota((16, 128), 1) * 8 + j).astype(F32)
    owner_at = jnp.sum(
        jnp.where(row_place >= ends, 1.0, 0.0), axis=0, keepdims=True
    ).astype(I32)
    slot_at = owner_at * 16 + (iota((1, 128), 1) & 15)
    rs[8:9, :] = slot_at
    request = iota((32, 128), 0) & 15
    position = iota((32, 128), 0) >> 4
    for r in range(16):
        position = position + jnp.where(request == r, lens[r], 0)
    lane32 = iota((32, 128), 1)
    angle = position.astype(F32) * turn_rate(lane32)
    ntab[0] = jnp.cos(angle)
    ntab[1] = jnp.where((lane32 & 63) < 32, -1.0, 1.0) * jnp.sin(angle)

    c_wd.wait()
    c_new.wait()
    c_uq = load(uq_h, uq, lsem.at[2])
    c_uk = load(uk_h, uk, lsem.at[3])
    npp[0] = nt(newh[...], wd[0:1152, :]).astype(BF16)
    npp[1, :, 0:896] = nt(newh[...], wd[1152:2048, :]).astype(BF16)
    tail = nt(newh[...], wd[2048:2112, :])
    npp[1, :, 896:1024] = jnp.concatenate([tail, tail], axis=1).astype(BF16)
    npp[1, :, 1024:1152] = jnp.zeros((32, 128), BF16)
    c_hid.wait()

    def k_copy(r):
        return pltpu.make_async_copy(cache_h.at[r], kc.at[r], ksem.at[r])

    @pl.loop(0, 16)
    def _(r):
        k_copy(r).start()

    c_uv = load(uv_h, uv, lsem.at[4])
    c_wo = load(wo_h, wo, lsem.at[5])
    @pl.loop(0, 2)
    def _(t):
        rows = pl.ds(pl.multiple_of(t * 512, 512), 512)
        h = hid[rows, :]
        part[rows, 0:512] = nt(h, wd[1536:2048, :]).astype(BF16)
        u = nt(h, wd[2048:2112, :])
        part[rows, 512:640] = jnp.concatenate([u, u], axis=1).astype(BF16)

    def npx_copy(dx):
        return remote(
            npx, npxr.at[dx], np_ss.at[dx], np_rs.at[dx], (i, 2 * ((x + dx) % 4) + c)
        )

    def permuted(first, second):
        ids = rs[0:8, :]
        top = [one_hot(sub128 == ids[b : b + 1, :] - first * 128) for b in range(8)]
        low = [one_hot(sub128 == ids[b : b + 1, :] - second * 128) for b in range(8)]
        pick = jnp.concatenate(
            [jnp.concatenate(top, axis=1), jnp.concatenate(low, axis=1)], axis=0
        )
        return nn(pick, part[...])

    def p_copy(dx):
        return remote(ps.at[dx], pr.at[dx], p_ss.at[dx], p_rs.at[dx], (i, sib))

    def via_copy(k):
        return remote(
            xs.at[2, pl.ds(64 * k, 64), :], xr.at[2, pl.ds(64 * k, 64), :],
            x_ss.at[k], x_rs.at[k], (i, 2 * ((x + 1 + 2 * k) % 4) + c),
        )

    def x_copy(dx, k):
        rows = pl.ds(64 * k, 64)
        return remote(
            xs.at[dx, rows, :], xr.at[dx, rows, :], x_ss.at[2 * dx + k], x_rs.at[2 * dx + k],
            (i, 2 * ((x + dx) % 4) + c),
        )

    @pl.loop(0, 2)
    def _(t):
        first, second = 2 + t, 1 - t
        both = permuted(2 * ((x + first) % 4) + 1 - c, 2 * ((x + second) % 4) + 1 - c)
        ps[first] = both[0:128].astype(BF16)
        ps[second] = both[128:256].astype(BF16)

    pl.semaphore_wait(barrier, 22)
    np_pair = remote(npp.at[1 - c], npair, np_ss.at[0], np_rs.at[0], (i, sib))
    np_pair.start()
    for dx in (2, 1, 3, 0):
        p_copy(dx).start()

    def t_copy(di):
        to = (i + di) % 16
        return remote(tsend.at[to], trecv.at[i], ts_sem.at[di], tr_sem.at[di], (to, j))

    @pl.loop(0, 2)
    def _(t):
        first, second = 2 + t, (1 - t) % 4
        both = permuted(2 * ((x + first) % 4) + c, 2 * ((x + second) % 4) + c)
        own[first] = both[0:128]
        own[second] = both[128:256]

        @pl.when(t == 0)
        def _():
            np_pair.wait_recv()
            npx[...] = (npp[c].astype(F32) + npair[...].astype(F32)).astype(BF16)
            for dx in (2, 1, 3):
                npx_copy(dx).start()
            p_copy(2).wait_recv()
            xs[2] = (own[2] + pr[2].astype(F32)).astype(BF16)
            via_copy(0).start()
            via_copy(1).start()
            for di in range(1, 16):
                t_copy(di).start()
            p_copy(1).wait_recv()
            own[1] = own[1] + pr[1].astype(F32)
            xs[1, 64:128, :] = own[1, 64:128, :].astype(BF16)
            x_copy(1, 1).start()

    p_copy(3).wait_recv()
    own[3] = own[3] + pr[3].astype(F32)
    xs[3, 0:64, :] = own[3, 0:64, :].astype(BF16)
    x_copy(3, 0).start()
    p_copy(0).wait_recv()
    own[0] = own[0] + pr[0].astype(F32)

    total = npx[...].astype(F32)
    for dx in (1, 3, 2):
        npx_copy(dx).wait_recv()
        total = total + npxr[dx].astype(F32)
    npfin[c] = total.astype(BF16)
    np_swap = remote(npfin.at[c], npfin.at[c], np_ss.at[4], np_rs.at[4], (i, sib))
    np_swap.start()
    via_copy(0).wait_recv()
    xs[1, 0:64, :] = (own[1, 0:64, :] + xr[2, 0:64, :].astype(F32)).astype(BF16)
    x_copy(1, 0).start()
    via_copy(1).wait_recv()
    xs[3, 64:128, :] = (own[3, 64:128, :] + xr[2, 64:128, :].astype(F32)).astype(BF16)
    x_copy(3, 1).start()
    np_swap_in = remote(npfin.at[1 - c], npfin.at[1 - c], np_ss.at[4], np_rs.at[4], (i, sib))
    np_swap_in.wait_recv()

    unit = LOG2E / (NOPE + ROPE) ** 0.5
    c_gq.wait()
    c_gkv.wait()
    low32 = iota((32, 128), 1) < 64
    q_in = jnp.concatenate([npfin[0], npfin[1, :, 0:384]], axis=1).astype(F32)
    q_in = q_in * lax.rsqrt(jnp.mean(q_in * q_in, axis=1, keepdims=True) + 1e-6) * gain_q[...].astype(F32).reshape(1, QRANK)
    qls[...] = q_in.astype(BF16)
    k_in = npfin[1, :, 384:896].astype(F32)
    k_in = k_in * lax.rsqrt(jnp.mean(k_in * k_in, axis=1, keepdims=True) + 1e-6) * gain_kv[...].astype(F32).reshape(1, LATENT)
    newk[0:32, 0:512] = k_in.astype(BF16)
    newk[32:128, 0:512] = jnp.zeros((96, 512), BF16)
    u = npfin[1, :, 896:1024].astype(F32)
    u = u * ntab[0] + turned(u) * ntab[1]
    row32 = iota((32, 128), 0)
    own_lane = lane32 == 64 + (row32 & 15)
    late = (lane32 == 83) & (row32 >= 16)
    u = jnp.where(low32, u, jnp.where(own_lane | late, 1.0, 0.0))
    newk[0:32, 512:640] = u.astype(BF16)
    newk[32:128, 512:640] = one_hot(iota((96, 128), 1) == 80)
    other = (lane32 >= 64) & (lane32 < 81) & jnp.logical_not(own_lane)
    qex = jnp.where(other | ((lane32 == 83) & (row32 < 16)), HIDE, 0.0)

    c_uq.wait()
    c_uk.wait()

    def two_heads(p):
        q = nn(qls[...], uq[:, pl.ds(pl.multiple_of(p * 384, 384), 384)])
        t0, t1, t2 = q[:, 0:128], q[:, 128:256], q[:, 256:384]
        odd = jnp.where(low32, pltpu.roll(t1, 64, 1), pltpu.roll(t2, 64, 1))
        rope = jnp.where(low32, t1, t2)
        rope = rope * ntab[0] + turned(rope) * ntab[1]
        for s, (nope, rot) in enumerate(((t0, rope), (odd, pltpu.roll(rope, 64, 1)))):
            rows = pl.ds(pl.multiple_of(p * 64 + s * 32, 32), 32)
            ql[rows, 0:512] = (nn(nope.astype(BF16), uk[2 * p + s]) * unit).astype(BF16)
            ql[rows, 512:640] = jnp.where(low32, rot * unit, qex).astype(BF16)

    @pl.loop(0, 4)
    def _(p):
        for q in range(2):
            two_heads(2 * p + q)

    @pl.loop(0, 2)
    def _(t):
        n = iota((256, 512), 0) + t * 256
        want = ((n & 31) >> 1) * 32 + (n & 1) * 16 + (n >> 5)
        rows = pl.ds(pl.multiple_of(t * 256, 256), 256)
        qs[rows, :] = nn(one_hot(iota((256, 512), 1) == want), ql[...]).astype(BF16)

    at_src = tsend[i]
    trecv[i] = at_src
    for di in range(1, 16):
        src = (i + 16 - di) % 16
        remote(tsend.at[src], trecv.at[src], ts_sem.at[di], tr_sem.at[di], (src, j)).wait_recv()

    tall, wide = [], []
    for s in range(16):
        cell = trecv[s, 0:1, :].astype(I32)
        tall.append(one_hot(sub128 == (cell >> 7)))
        wide.append(one_hot(sub128 == (cell & 127)))
    taken = nt(jnp.concatenate(tall, axis=1), jnp.concatenate(wide, axis=1))
    length = jnp.zeros((128, 128), I32)
    weigh = jnp.where(iota((8, 128), 1) == 81, -128.0, 0.0)
    weigh = jnp.where(iota((8, 128), 1) == 82, -1.0, weigh)
    for r in range(16):
        length = length + jnp.where((sub128 >> 3) == r, lens[r], 0)
        weigh = weigh + jnp.where(iota((8, 128), 1) == 64 + r, lens[r], 0).astype(F32)
    seen = (sub128 & 7) * 128 + lane128 < length
    biasm[...] = jnp.where((taken < 0.5) & seen, 0.0, HIDE)

    snew[...] = nt(qs[...], newk[...])
    quarter = [one_hot((lane128 >> 5) == r) for r in range(4)]

    def cache_four(t):
        if True:
            for r in range(4):
                k_copy(4 * t + r).wait()
            rows = pl.ds(pl.multiple_of(t * 128, 128), 128)
            bias = biasm[pl.ds(pl.multiple_of(t * 32, 32), 32), :]
            s = [
                nn(qs[pl.ds(pl.multiple_of(t * 128 + r * 32, 32), 32), 0:576], kc[4 * t + r])
                for r in range(4)
            ]
            s = [
                jnp.concatenate(
                    [
                        s[r][:, g * 128 : (g + 1) * 128] + bias[8 * r + g : 8 * r + g + 1, :]
                        for r in range(4)
                    ],
                    axis=0,
                )
                for g in range(8)
            ]
            s.append(snew[rows, :])
            top = jnp.max(functools.reduce(jnp.maximum, s), axis=1, keepdims=True)
            m = jnp.broadcast_to(top, (128, 128))
            e = [jnp.exp2(v - m) for v in s]
            m_s[rows, :] = m
            l_s[rows, :] = functools.reduce(jnp.add, e)
            enew[rows, :] = e[8].astype(BF16)
            e = [v.T.astype(BF16) for v in e[0:8]]
            val = functools.reduce(
                jnp.add,
                [
                    nn(kc[4 * t + r, 0:512, :], jnp.concatenate([v * quarter[r] for v in e], axis=0))
                    for r in range(4)
                ],
            )
            acc[rows, :] = val.T

    total = own[0]
    for dx in (1, 3):
        x_copy(dx, 0).wait_recv()
        x_copy(dx, 1).wait_recv()
        total = total + xr[dx].astype(F32)
    lat = total[:, 0:512]
    lat = lat * lax.rsqrt(jnp.mean(lat * lat, axis=1, keepdims=True) + 1e-6) * gain_kv[...].astype(F32).reshape(1, LATENT)
    tail = total[:, 512:640]
    marks = feat[...]
    at = jnp.where(lane128 == 81, 128.0, jnp.where(lane128 == 82, 1.0, 0.0))
    at = jnp.sum(marks * at, axis=1, keepdims=True)
    angle = at * turn_rate(lane128)
    sign = jnp.where((lane128 & 63) < 32, -1.0, 1.0)
    tail = tail * jnp.cos(angle) + turned(tail) * (sign * jnp.sin(angle))
    tail = jnp.where(lane128 < 64, tail, marks)
    rows_b = jnp.concatenate([lat, tail], axis=1).astype(BF16)
    spread = one_hot(iota((256, 128), 0) == rs[8:9, :])
    disp[...] = nn(spread, rows_b).astype(BF16)

    def d_copy(di):
        to = (i + di) % 16
        return remote(
            disp.at[pl.ds(pl.multiple_of(to * 16, 16), 16), :],
            slots.at[j, pl.ds(pl.multiple_of(i * 16, 16), 16), :],
            d_ss.at[di], d_rs.at[di], (to, j),
        )

    for di in range(1, 16):
        d_copy(di).start()
    at_me = pl.ds(pl.multiple_of(i * 16, 16), 16)
    slots[j, at_me, :] = disp[at_me, :]


    def g_half(block, k):
        return slots.at[block, pl.ds(128 * k, 128), :]

    def g_copy(block, k, ss, to):
        return remote(
            g_half(block, k), g_half(block, k), g_ss.at[ss], g_rs.at[block, k], (i, to)
        )

    def g_wait(block, k):
        g_copy(block, k, 0, sib).wait_recv()

    above, below, across = (2 * ((x + d) % 4) + c for d in (1, 3, 2))
    g_sent = []

    def g_send(block, k, to):
        g_sent.append((block, k, len(g_sent), to))
        g_copy(*g_sent[-1]).start()

    @pl.loop(0, 4)
    def _(t):
        cache_four(t)

        @pl.when(t == 0)
        def _():
            for di in range(1, 16):
                src = (i + 16 - di) % 16
                remote(
                    disp.at[pl.ds(pl.multiple_of(src * 16, 16), 16), :],
                    slots.at[j, pl.ds(pl.multiple_of(src * 16, 16), 16), :],
                    d_ss.at[di], d_rs.at[di], (src, j),
                ).wait_recv()
            marks = slots[j, :, 512:640].astype(F32)
            left = jnp.sum(marks * weigh[0:1, :], axis=1, keepdims=True)
            marks = jnp.where(
                iota((256, 128), 1) == 80, jnp.where(left > 0.5, 0.0, 1.0), marks
            )
            slots[j, :, 512:640] = marks.astype(BF16)
            g_send(j, 0, above)
            g_send(j, 1, below)
            g_send(j, 0, sib)
            g_send(j, 1, sib)

        @pl.when(t == 1)
        def _():
            g_copy(*g_sent[0]).wait_send()
            g_copy(*g_sent[1]).wait_send()
            g_send(j, 1, above)
            g_send(j, 0, below)

        @pl.when(t == 2)
        def _():
            g_wait(below, 0)
            g_send(below, 0, above)
            g_wait(above, 1)
            g_send(above, 1, below)
            g_send(below, 0, sib)
            g_send(above, 1, sib)

    acc[...] = acc[...] + nn(enew[...], newk[:, 0:512])

    def slot_part(first, second):
        q = qs[...]
        blocks = (first, second)
        s = [nt(q, slots[b]) for b in blocks]
        s = [v[:, g * 128 : (g + 1) * 128] for v in s for g in range(2)]
        old = m_s[...]
        top = jnp.max(functools.reduce(jnp.maximum, s), axis=1, keepdims=True)
        m = jnp.maximum(old, jnp.broadcast_to(top, (512, 128)))
        keep = jnp.exp2(old - m)
        e = [jnp.exp2(v - m) for v in s]
        m_s[...] = m
        l_s[...] = l_s[...] * keep + functools.reduce(jnp.add, e)
        e = [v.astype(BF16) for v in e]
        val = nn(jnp.concatenate(e[0:2], axis=1), slots[first, :, 0:512])
        val = val + nn(jnp.concatenate(e[2:4], axis=1), slots[second, :, 0:512])
        acc[...] = acc[...] * jnp.concatenate([keep] * 4, axis=1) + val

    @pl.loop(0, 4)
    def _(t):
        @pl.when(t == 1)
        def _():
            g_wait(below, 1)
            g_send(below, 1, sib)
            g_wait(above, 0)
            g_send(above, 0, sib)

        @pl.when(t == 3)
        def _():
            for k in range(2):
                g_wait(across, k)
                g_send(across, k, sib)

        chip = 2 * ((x + jnp.where(t == 1, 3, jnp.where(t == 2, 1, jnp.where(t == 3, 2, 0)))) % 4)
        for k in range(2):
            g_wait(chip + 1 - c, k)
        slot_part(chip + c, chip + 1 - c)

    @pl.loop(0, 2)
    def _(t):
        rows = pl.ds(pl.multiple_of(t * 256, 256), 256)
        ob[rows, :] = (
            acc[rows, :] * (1.0 / jnp.sum(l_s[rows, :], axis=1, keepdims=True))
        ).astype(BF16)

    @pl.loop(0, 2)
    def _(t):
        n = iota((256, 512), 0) + t * 256
        want = (n & 15) * 32 + (n >> 5) * 2 + ((n >> 4) & 1)
        rows = pl.ds(pl.multiple_of(t * 256, 256), 256)
        op[rows, :] = nn(one_hot(iota((256, 512), 1) == want), ob[...]).astype(BF16)

    c_uv.wait()
    c_wo.wait()

    def o_dev(dz, dy):
        return ((z + dz) % 4) * 4 + (y + dy) % 4

    def near(half, d):
        return o_dev(0, d) if half == 0 else o_dev(d, 0)

    def far(half, d):
        return o_dev(d, 0) if half == 0 else o_dev(0, d)

    def cross(half, n, f):
        return o_dev(f, n) if half == 0 else o_dev(n, f)

    h_sent = []

    def h_copy(half, piece, k, ss, to):
        ref = hog.at[half, piece, pl.ds(16 * k, 16), :]
        return remote(ref, ref, h_ss.at[ss], h_rs.at[half, piece, k], (to, j))

    def h_send(half, piece, k, to):
        cp = h_copy(half, piece, k, len(h_sent), to)
        cp.start()
        h_sent.append(cp)

    def h_wait(half, piece, k):
        h_copy(half, piece, k, 0, i).wait_recv()

    def far_first(half, piece):
        h_send(half, piece, 0, far(half, 1))
        h_send(half, piece, 1, far(half, 3))

    def far_rest(half, piece):
        h_send(half, piece, 1, far(half, 1))
        h_send(half, piece, 0, far(half, 3))

    def far_on(half, n):
        h_wait(half, cross(half, n, 3), 0)
        h_send(half, cross(half, n, 3), 0, far(half, 1))
        h_wait(half, cross(half, n, 1), 1)
        h_send(half, cross(half, n, 1), 1, far(half, 3))

    def far_end(half, n, f):
        if f != 1:
            h_wait(half, cross(half, n, f), 1)
        if f != 3:
            h_wait(half, cross(half, n, f), 0)

    halves = range(2)
    for half in halves:

        @pl.loop(0, 2)
        def _(t):
            for h in range(4):
                at = t * 4 + h
                rows = pl.ds(pl.multiple_of((half * 8 + at) * 32, 32), 32)
                hog[half, i, :, pl.ds(pl.multiple_of(at * 128, 128), 128)] = nn(
                    op[rows, :], uv[half * 8 + at]
                ).astype(BF16)

        h_send(half, i, 0, near(half, 1))
        h_send(half, i, 1, near(half, 3))
        h_send(half, i, 1, near(half, 1))
        h_send(half, i, 0, near(half, 3))
    for half in halves:
        far_first(half, i)
    for half in halves:
        h_wait(half, near(half, 3), 0)
        h_send(half, near(half, 3), 0, near(half, 1))
        h_wait(half, near(half, 1), 1)
        h_send(half, near(half, 1), 1, near(half, 3))
    for half in halves:
        h_wait(half, near(half, 3), 1)
        far_first(half, near(half, 3))
        h_wait(half, near(half, 1), 0)
        far_first(half, near(half, 1))
    for half in halves:
        far_on(half, 0)
    for half in halves:
        far_rest(half, i)
    for half in halves:
        h_wait(half, near(half, 2), 0)
        h_wait(half, near(half, 2), 1)
        far_first(half, near(half, 2))
    for n in (3, 1):
        for half in halves:
            far_on(half, n)
    for n in (3, 1):
        for half in halves:
            far_rest(half, near(half, n))
    for half in halves:
        far_on(half, 2)
    for half in halves:
        far_rest(half, near(half, 2))

    def o_pair(t):
        return remote(opair.at[t], opin.at[t], op_ss.at[t], op_rs.at[t], (i, sib))

    def o_copy(t, to):
        return remote(osend.at[t], orecv.at[x], o_ss.at[t], o_rs.at[x], (i, 2 * to + c))

    def columns(t, row):
        four = pl.ds(row * 4, 4)
        res = nt(hog[0, four].reshape(128, 1024), wo[:, 0:1024])
        res = res + nt(hog[1, four].reshape(128, 1024), wo[:, 1024:2048])
        ores[t, :, 0:448] = res
        opair[t, :, 0:448] = ores[t, pl.ds(pl.multiple_of((1 - c) * 64, 64), 64), 0:448].astype(
            BF16
        )
        o_pair(t).start()

    def onward(t, row):
        o_pair(t).wait_recv()
        own_half = ores[t, pl.ds(pl.multiple_of(c * 64, 64), 64), :]
        osend[t] = (own_half + opin[t].astype(F32)).astype(BF16)

        @pl.when(row != x)
        def _():
            o_copy(t, row).start()

        @pl.when(row == x)
        def _():
            orecv[x] = osend[t]

    order = (0, 3, 1, 2)
    rows_at = [(z + dz) % 4 for dz in order]
    @pl.loop(0, 4)
    def _(t):
        for at, d in enumerate(order):

            @pl.when(t == at)
            def _():
                if d != 0:
                    for n in range(4):
                        far_end(0, n, d)
                for f in (1, 3, 2):
                    far_end(1, d, f)

        step = jnp.where(t == 1, 3, jnp.where(t == 2, 1, jnp.where(t == 3, 2, 0)))
        row = (z + step) % 4
        columns(t, row)
        onward(t, row)

    total = jnp.zeros((64, 448), F32)
    for dx in range(1, 4):
        src = (x + dx) % 4
        remote(osend.at[0], orecv.at[src], o_ss.at[0], o_rs.at[src], (i, 2 * src + c)).wait_recv()
    for src in range(4):
        total = total + orecv[src, :, 0:448].astype(F32)
    total = total.astype(BF16)
    for o in range(2):
        for s in range(2):
            out[s, o * 16 : (o + 1) * 16, :] = total[o * 32 + s * 16 : o * 32 + s * 16 + 16, :]

    for di in range(1, 16):
        t_copy(di).wait_send()
        d_copy(di).wait_send()
    np_pair.wait_send()
    np_swap.wait_send()
    for dx in range(4):
        p_copy(dx).wait_send()
    for dx in range(1, 4):
        npx_copy(dx).wait_send()
    for k in range(2):
        x_copy(1, k).wait_send()
        x_copy(3, k).wait_send()
        via_copy(k).wait_send()
    for one in g_sent[2:]:
        g_copy(*one).wait_send()
    for cp in h_sent:
        cp.wait_send()
    for t in range(4):
        o_pair(t).wait_send()

        @pl.when(rows_at[t] != x)
        def _():
            o_copy(t, rows_at[t]).wait_send()


def local(
    prompt_hidden, owner, offsets, cache, lengths, new_hidden, w_down,
    gain_q, gain_kv, w_uq, w_uk, w_uv, w_out,
):
    vm = pl.BlockSpec(memory_space=pltpu.VMEM)
    hb = pl.BlockSpec(memory_space=pl.ANY)
    V = pltpu.VMEM
    S = pltpu.SemaphoreType.DMA
    scratch = [
        V((8, 128), I32), V((8, 128), I32), V((QRANK,), BF16), V((LATENT,), BF16), V((32, 896), BF16),
        V((1024, 896), BF16), V((2112, 896), BF16), V((1536, 3072), BF16), V((16, 128, 512), BF16),
        V((16, 576, 1024), BF16), V((16, 512, 128), BF16), V((448, 2048), BF16), S((11,)), S((16,)),
        V((16, 128), I32), V((128, 128), F32), V((16, 8, 128), F32), V((16, 8, 128), F32), S((16,)), S((16,)),
        V((2, 32, 1152), BF16), V((32, 1152), BF16), V((32, 1152), BF16), V((4, 32, 1152), BF16),
        V((2, 32, 1152), BF16), S((5,)), S((5,)), V((2, 32, 128), F32),
        V((1024, 640), BF16), V((4, 128, 640), BF16), V((4, 128, 640), BF16),
        V((4, 128, 640), BF16), V((4, 128, 640), BF16), V((4, 128, 640), F32),
        S((4,)), S((4,)), S((8,)), S((8,)),
        V((256, 640), BF16), V((8, 256, 640), BF16), S((16,)), S((16,)), S((14,)), S((8, 2)),
        V((32, 1536), BF16), V((512, 640), BF16), V((512, 640), BF16), V((128, 640), BF16),
        V((512, 128), F32), V((512, 128), BF16), V((128, 128), F32), V((512, 512), F32), V((512, 128), F32), V((512, 128), F32),
        V((512, 512), BF16), V((512, 512), BF16),
        V((2, 16, 32, 1024), BF16), S((60,)), S((2, 16, 2)),
        V((4, 128, 512), F32), V((4, 64, 512), BF16), V((4, 64, 512), BF16), S((4,)), S((4,)),
        V((4, 64, 512), BF16), V((4, 64, 512), BF16), S((4,)), S((4,)),
    ]
    return pl.pallas_call(
        kernel,
        out_shape=jax.ShapeDtypeStruct((2, 32, 448), BF16),
        in_specs=[pl.BlockSpec(memory_space=pltpu.SMEM)] + [hb] * 12,
        out_specs=vm,
        scratch_shapes=scratch,
        compiler_params=pltpu.CompilerParams(
            collective_id=0, has_side_effects=True, vmem_limit_bytes=60 * 1024 * 1024
        ),
    )(
        lengths, owner.reshape(8, 128), offsets.reshape(8, 128),
        gain_q, gain_kv,
        new_hidden.reshape(32, 896),
        prompt_hidden, w_down.T, w_uq, w_uk, jnp.swapaxes(cache, 1, 2), w_uv, w_out.T,
    )


def solution(mesh):
    in_specs = (
        P("seq", "head"), P("seq", None), P("seq"), P("seq", None, None), P("seq"),
        P(None, "seq", "head"), P("head", None), P(), P(), P(None, "head"),
        P("head", None, None), P("head", None, None), P("head", "seq"),
    )
    return jax.shard_map(
        local, mesh=mesh, in_specs=in_specs, out_specs=P(None, "head", "seq"), check_vma=False
    )
```
